256 devices in a mesh: row: 8 (over y, x_hi), pair: 32 (over z, x_lo, core).
Axes of the slice: x: 4 (x_hi: 2, x_lo: 2; x = x_hi * 2 + x_lo), y: 4, z: 8, core: 2. Of those that a mesh axis runs over, the one named last changes fastest.
Arguments:
- top_blocks: float32 [16384, 8192], P('row', 'pair'), may hold values from -60 to 60, as said below
- bottom_blocks: float32 [16384, 8192], P('row', 'pair'), may hold values from -60 to 60, as said below
Outputs:
- top_out: float32 [16384, 8192], P('row', 'pair')
- bottom_out: float32 [16384, 8192], P('row', 'pair')
The draws below stay inside these ranges and needn't reach their ends.
Inputs may be any that keep to these rules, and one draw needn't show every extreme that they name: `top_blocks`: entries of the slab. `bottom_blocks`: entries of the slab.
All inputs are finite; a program needn't handle non-finite values.
Results may differ from the reference program's by a relative error of at most 0.00015.
Values sent between devices are 32-bit elements; how exact they have to be, the bound alone decides.
No kernel may reach another device: no remote copies, remote signals or barrier semaphores. Data moves between devices by JAX's collectives and lax.ppermute only.
A program may use at most 64 MiB of HBM per device.

```python
import math
import jax
import jax.numpy as jnp
from jax import lax

B = 256
STEPS = 2
SWEEPS = 3
M = 16384
N_PAIR = 32


def draw_top_blocks(key, part):
    key = jax.random.fold_in(key, 11)
    key_a, key_b = jax.random.split(key, 2)
    shape_rc = (M, B * N_PAIR)
    col_scale = 0.3 * jnp.exp(jax.random.uniform(key_b, (1, B * N_PAIR), dtype=jnp.float32) * math.log(10.0))
    entries = jnp.clip(jax.random.normal(key_a, shape_rc, dtype=jnp.float32), -4.0, 4.0)
    return (entries * col_scale).astype(jnp.float32)


def draw_bottom_blocks(key, part):
    key = jax.random.fold_in(key, 23)
    key_a, key_b = jax.random.split(key, 2)
    shape_rc = (M, B * N_PAIR)
    col_scale = 0.3 * jnp.exp(jax.random.uniform(key_b, (1, B * N_PAIR), dtype=jnp.float32) * math.log(10.0))
    entries = jnp.clip(jax.random.normal(key_a, shape_rc, dtype=jnp.float32), -4.0, 4.0)
    return (entries * col_scale).astype(jnp.float32)


def setup_inputs(seed: int = 0) -> dict:
    splits = jax.random.split(jax.random.key(seed), 3)
    top_blocks = draw_top_blocks(jax.random.fold_in(splits[2], 71), 0)
    bottom_blocks = draw_bottom_blocks(jax.random.fold_in(splits[2], 71), 0)
    return {"top_blocks": top_blocks, "bottom_blocks": bottom_blocks}


def matmul_hi(left, right):
    return jnp.dot(left, right, preferred_element_type=jnp.float32, precision=lax.Precision.HIGHEST)

def rotation(gram_mat):
    width_n = gram_mat.shape[0]
    col_sq = jnp.diagonal(gram_mat) + 1e-06
    corr_mat = gram_mat / jnp.sqrt(col_sq[:, None] * col_sq[None, :])
    skew_mat = (col_sq[None, :] - col_sq[:, None]) / (col_sq[None, :] + col_sq[:, None])
    generator = corr_mat * skew_mat
    frobenius = jnp.sqrt(jnp.sum(generator * generator))
    identity = jnp.eye(width_n, dtype=jnp.float32)
    rotate = identity + generator / (1.0 + frobenius)
    for sweep_idx in range(SWEEPS):
        inner_mat = matmul_hi(rotate.T, rotate)
        rotate = matmul_hi(rotate, 1.5 * identity - 0.5 * inner_mat)
    return rotate

def pair_step(blocks):
    joined = jnp.concatenate([blocks[0], blocks[1]], axis=1)
    gram_mat = matmul_hi(joined.T, joined)
    rotated = matmul_hi(joined, rotation(gram_mat))
    return (rotated[:, :B], rotated[:, B:])

def reference(top_blocks, bottom_blocks):
    rows_m = top_blocks.shape[0]
    top_set = top_blocks.reshape(rows_m, N_PAIR, B).transpose(1, 0, 2)
    bottom_set = bottom_blocks.reshape(rows_m, N_PAIR, B).transpose(1, 0, 2)
    for step_idx in range(STEPS):
        new_top, bottom_set = lax.map(pair_step, (top_set, bottom_set))
        top_set = jnp.roll(new_top, 1, axis=0)
    top_out = top_set.transpose(1, 0, 2).reshape(rows_m, N_PAIR * B)
    bottom_out = bottom_set.transpose(1, 0, 2).reshape(rows_m, N_PAIR * B)
    return (top_out, bottom_out)
```

```python
import functools

import jax
import jax.numpy as jnp
from jax import lax
from jax.experimental import pallas as pl
from jax.experimental.pallas import tpu as pltpu
from jax.sharding import PartitionSpec as P

STEPS = 2
SWEEPS = 3
W = 256
H = 128
PIECE = 2 * H + 8
CHUNK = 512
BF, F32 = jnp.bfloat16, jnp.float32
VMEM_LIMIT = 48 * 1024 * 1024


def split2(x):
    high = x.astype(BF)
    return high, (x - high.astype(F32)).astype(BF)


def dot_tn(left, right):
    return lax.dot_general(left, right, (((0,), (0,)), ((), ())), preferred_element_type=F32)


def dot_nn(left, right):
    return jnp.dot(left, right, preferred_element_type=F32)


def mm3(left, right):
    lh, ll = left
    rh, rl = right
    return dot_nn(lh, rh) + (dot_nn(lh, rl) + dot_nn(ll, rh))


def mm1(left, right):
    return dot_nn(left[0], right[0])


def iotas(shape):
    return lax.broadcasted_iota(jnp.int32, shape, 0), lax.broadcasted_iota(jnp.int32, shape, 1)


def gram_kernel(where_ref, top_ref, bottom_ref, *refs):
    outs, (xtt, ytt, xbb, ybb, tb, pieces) = refs[:4], refs[4:]
    step = pl.program_id(0)

    @pl.when(step == 0)
    def _():
        for acc in (xtt, ytt, xbb, ybb, tb):
            acc[...] = jnp.zeros_like(acc)

    th, tl = split2(top_ref[...])
    bh, bl = split2(bottom_ref[...])
    xtt[...] += dot_tn(th, th)
    ytt[...] += dot_tn(th, tl)
    xbb[...] += dot_tn(bh, bh)
    ybb[...] += dot_tn(bh, bl)
    tb[...] += dot_tn(th, bh) + (dot_tn(th, bl) + dot_tn(tl, bh))

    @pl.when(step == pl.num_programs(0) - 1)
    def _():
        row, col = iotas((H, H))
        upper, diag = row <= col, row == col
        for idx, (x, y) in enumerate(((xtt, ytt), (xbb, ybb))):
            full = x[...] + (y[...] + y[...].T)
            first, last = full[:H, :H], full[H:, H:]
            pieces[idx, 0:H] = full[:H, H:]
            pieces[idx, H:2 * H] = jnp.where(upper, first, last)
            line = jnp.sum(jnp.where(diag, last, 0.0), axis=0, keepdims=True)
            pieces[idx, 2 * H:PIECE] = jnp.broadcast_to(line, (8, H))
        for idx in range(2):
            half = tb[idx * H:(idx + 1) * H, :]
            pieces[2 + idx, 0:H] = half[:, :H]
            pieces[2 + idx, H:2 * H] = half[:, H:]
            pieces[2 + idx, 2 * H:PIECE] = jnp.zeros((8, H), F32)
        mine = where_ref[0]
        for ahead in range(4):
            outs[ahead][...] = pieces[(mine + ahead) % 4]


def gram_pieces(where, top, bottom):
    rows = top.shape[0]
    piece = jax.ShapeDtypeStruct((PIECE, H), F32)
    square = pltpu.VMEM((W, W), F32)
    return pl.pallas_call(
        gram_kernel,
        out_shape=[piece] * 4,
        grid_spec=pltpu.PrefetchScalarGridSpec(
            num_scalar_prefetch=1,
            grid=(rows // CHUNK,),
            in_specs=[pl.BlockSpec((CHUNK, W), lambda i, *_: (i, 0))] * 2,
            out_specs=[pl.BlockSpec((PIECE, H), lambda i, *_: (0, 0))] * 4,
            scratch_shapes=[square] * 5 + [pltpu.VMEM((4, PIECE, H), F32)],
        ),
        compiler_params=pltpu.CompilerParams(vmem_limit_bytes=VMEM_LIMIT),
        cost_estimate=pl.CostEstimate(flops=7 * 2 * W * W * rows, bytes_accessed=8 * W * rows, transcendentals=0),
    )(where, top, bottom)


def rotation_kernel(where_ref, q0, q1, q2, q3, high_ref, low_ref, pieces, gram):
    mine = where_ref[0]
    for behind, piece in enumerate((q0, q1, q2, q3)):
        pieces[(mine + 4 - behind) % 4] = piece[...]
    row, col = iotas((H, H))
    upper, diag = row <= col, row == col

    def put(i, j, block):
        gram[i * H:(i + 1) * H, j * H:(j + 1) * H] = block

    lines, columns = [], []
    for half in range(2):
        off = pieces[half, 0:H]
        both = pieces[half, H:2 * H]
        line = pieces[half, 2 * H:2 * H + 1]
        turned = both.T
        first = jnp.where(upper, both, turned)
        last = jnp.where(diag, line, jnp.where(upper, turned, both))
        a, b = 2 * half, 2 * half + 1
        put(a, b, off)
        put(b, a, off.T)
        put(a, a, first)
        put(b, b, last)
        for block in (first, last):
            on = jnp.where(diag, block, 0.0)
            lines.append(jnp.sum(on, axis=0, keepdims=True))
            columns.append(jnp.sum(on, axis=1, keepdims=True))
    for i in range(2):
        for j in range(2):
            block = pieces[2 + i, j * H:(j + 1) * H]
            put(i, 2 + j, block)
            put(2 + j, i, block.T)
    sq_line = jnp.concatenate(lines, axis=1) + 1e-06
    sq_col = jnp.concatenate(columns, axis=0) + 1e-06
    generator = gram[...] / jnp.sqrt(sq_col * sq_line) * ((sq_line - sq_col) / (sq_line + sq_col))
    frobenius = jnp.sqrt(jnp.sum(generator * generator))
    skew = generator * (1.0 / (1.0 + frobenius))

    s2 = split2(skew)
    n = -mm3(s2, s2)
    n_2 = split2(n)
    nn = mm3(n_2, n_2)
    d1 = 0.25 * mm3(split2(nn), n_2) - 0.75 * nn
    d1_2 = split2(d1)
    dd = mm1(d1_2, d1_2)
    d2 = 0.25 * mm1(split2(dd), d1_2) - 0.75 * dd
    x = 0.5 * (d1 + d2) - 0.25 * mm1(d1_2, split2(d2))
    y = 0.5 * n + x - 0.5 * mm3(n_2, split2(x))
    row, col = iotas((2 * W, 2 * W))
    rotate = jnp.where(row == col, 1.0, skew) - (y + mm3(s2, split2(y)))
    high, low = split2(rotate)
    high_ref[...] = high
    low_ref[...] = low


def rotation(where, quarters):
    half = jax.ShapeDtypeStruct((2 * W, 2 * W), BF)
    return pl.pallas_call(
        rotation_kernel,
        out_shape=[half, half],
        in_specs=[pl.BlockSpec(memory_space=pltpu.SMEM)] + [pl.BlockSpec(memory_space=pltpu.VMEM)] * 4,
        out_specs=[pl.BlockSpec(memory_space=pltpu.VMEM)] * 2,
        scratch_shapes=[pltpu.VMEM((4, PIECE, H), F32), pltpu.VMEM((2 * W, 2 * W), F32)],
        compiler_params=pltpu.CompilerParams(vmem_limit_bytes=VMEM_LIMIT),
        cost_estimate=pl.CostEstimate(flops=18 * 2 * (2 * W) ** 3, bytes_accessed=2 ** 21, transcendentals=0),
    )(where, *quarters)


def apply_kernel(top_ref, bottom_ref, high_ref, low_ref, out_ref):
    high, low = high_ref[...], low_ref[...]
    top, bottom = split2(top_ref[...]), split2(bottom_ref[...])
    out_ref[...] = mm3(top, (high[:W], low[:W])) + mm3(bottom, (high[W:], low[W:]))


def rotated(top, bottom, rotate, part, start, rows):
    first = start // CHUNK
    block = pl.BlockSpec((CHUNK, W), lambda i: (first + i, 0))
    turn = pl.BlockSpec((2 * W, W), lambda i: (0, part))
    return pl.pallas_call(
        apply_kernel,
        out_shape=jax.ShapeDtypeStruct((rows, W), F32),
        grid=(rows // CHUNK,),
        in_specs=[block, block, turn, turn],
        out_specs=pl.BlockSpec((CHUNK, W), lambda i: (i, 0)),
        compiler_params=pltpu.CompilerParams(vmem_limit_bytes=VMEM_LIMIT),
        cost_estimate=pl.CostEstimate(flops=6 * 2 * W * W * rows, bytes_accessed=12 * W * rows, transcendentals=0),
    )(top, bottom, *rotate)


def passed_along(array, by):
    length = lax.axis_size("pair")
    return lax.ppermute(array, "pair", [(i, (i + by) % length) for i in range(length)])


def along_y(array, by):
    length = lax.axis_size("row") // 2
    return lax.ppermute(
        array, "row", [(2 * y + h, 2 * ((y + by) % length) + h) for y in range(length) for h in range(2)]
    )


def across_x(array):
    return lax.ppermute(array, "row", [(i, i ^ 1) for i in range(lax.axis_size("row"))])


def summed_quarters(pieces):
    total = pieces[0] + along_y(pieces[1], 1) + along_y(pieces[2], 2) + along_y(pieces[3], 3)
    total = total + across_x(total)
    return [total, along_y(total, 1), along_y(total, 2), along_y(total, 3)]


def on_device(top, bottom):
    where = (lax.axis_index("row") // 2).astype(jnp.int32).reshape(1)
    rows = top.shape[0]
    for step_idx in range(STEPS):
        quarters = summed_quarters(gram_pieces(where, top, bottom))
        rotate = rotation(where, quarters)
        if step_idx < STEPS - 1:
            parts = [
                passed_along(rotated(top, bottom, rotate, 0, start, CHUNK), 1) for start in range(0, rows, CHUNK)
            ]
            bottom = rotated(top, bottom, rotate, 1, 0, rows)
            top = jnp.concatenate(parts)
        else:
            sent = passed_along(rotated(top, bottom, rotate, 0, 0, rows), 1)
            bottom = rotated(top, bottom, rotate, 1, 0, rows)
            top = sent
    return (top, bottom)


def solution(mesh):
    placed = (P("row", "pair"), P("row", "pair"))
    return jax.shard_map(on_device, mesh=mesh, in_specs=placed, out_specs=placed, check_vma=False)
```

```python
import functools

import jax
import jax.numpy as jnp
from jax import lax
from jax.experimental import pallas as pl
from jax.experimental.pallas import tpu as pltpu
from jax.sharding import PartitionSpec as P

STEPS = 2
SWEEPS = 3
W = 256
H = 128
PIECE = 2 * H + 8
Q = W // 4
CROSS = Q + 8
RAW = 512
MORE = 256
LAST = 768
BLOCK = 256
BF, F32 = jnp.bfloat16, jnp.float32
IN_VMEM = pl.BlockSpec(memory_space=pltpu.VMEM)
IN_SMEM = pl.BlockSpec(memory_space=pltpu.SMEM)
IN_HBM = pl.BlockSpec(memory_space=pltpu.HBM)
ANYWHERE = pl.BlockSpec(memory_space=pl.ANY)
MIB = 1024 * 1024


def granted(mib):
    return pltpu.CompilerParams(vmem_limit_bytes=mib * MIB)


def split2(x):
    high = x.astype(BF)
    return high, (x - high.astype(F32)).astype(BF)


def dot_tn(left, right):
    return lax.dot_general(left, right, (((0,), (0,)), ((), ())), preferred_element_type=F32)


def dot_nn(left, right):
    return jnp.dot(left, right, preferred_element_type=F32)


def mm3(left, right):
    lh, ll = left
    rh, rl = right
    return dot_nn(lh, rh) + (dot_nn(lh, rl) + dot_nn(ll, rh))


def mm1(left, right):
    return dot_nn(left[0], right[0])


def iotas(shape):
    return lax.broadcasted_iota(jnp.int32, shape, 0), lax.broadcasted_iota(jnp.int32, shape, 1)


def add_rows(accs, top, bottom, begin):
    th, tl = split2(top)
    bh, bl = split2(bottom)
    shares = (
        dot_tn(th, th),
        dot_tn(th, tl),
        dot_tn(bh, bh),
        dot_tn(bh, bl),
        dot_tn(th, bh) + (dot_tn(th, bl) + dot_tn(tl, bh)),
    )
    for acc, share in zip(accs, shares):
        acc[...] = share if begin else acc[...] + share


def put_pieces(accs, pieces, outs, mine):
    xtt, ytt, xbb, ybb, tb = accs
    row, col = iotas((H, H))
    upper, diag = row <= col, row == col
    for idx, (x, y) in enumerate(((xtt, ytt), (xbb, ybb))):
        full = x[...] + (y[...] + y[...].T)
        first, last = full[:H, :H], full[H:, H:]
        pieces[idx, 0:H] = full[:H, H:]
        pieces[idx, H:2 * H] = jnp.where(upper, first, last)
        line = jnp.sum(jnp.where(diag, last, 0.0), axis=0, keepdims=True)
        pieces[idx, 2 * H:PIECE] = jnp.broadcast_to(line, (8, H))
    for idx in range(2):
        half = tb[idx * H:(idx + 1) * H, :]
        pieces[2 + idx, 0:H] = half[:, :H]
        pieces[2 + idx, H:2 * H] = half[:, H:]
        pieces[2 + idx, 2 * H:PIECE] = jnp.zeros((8, H), F32)
    for ahead in range(4):
        outs[ahead][...] = pieces[(mine + ahead) % 4]


ACCS = [pltpu.VMEM((W, W), F32)] * 5
PIECES = pltpu.VMEM((4, PIECE, H), F32)


def load_kernel(top_ref, bottom_ref, out_ref, sems):
    rows = out_ref.shape[0] // 2
    copies = [
        pltpu.make_async_copy(ref.at[pl.ds(0, rows)], out_ref.at[pl.ds(side * rows, rows)], sems.at[side])
        for side, ref in enumerate((top_ref, bottom_ref))
    ]
    for copy in copies:
        copy.start()
    for copy in copies:
        copy.wait()


def loaded(top, bottom, rows):
    return pl.pallas_call(
        load_kernel,
        out_shape=jax.ShapeDtypeStruct((2 * rows, W), F32),
        in_specs=[IN_HBM, IN_HBM],
        out_specs=IN_VMEM,
        scratch_shapes=[pltpu.SemaphoreType.DMA((2,))],
        compiler_params=granted(51),
        cost_estimate=pl.CostEstimate(flops=0, bytes_accessed=16 * W * rows, transcendentals=0),
    )(top, bottom)


def first_gram_kernel(where_ref, loaded_ref, top_ref, bottom_ref, *refs):
    outs, rest, accs, pieces, sems = refs[:4], refs[4], refs[5:10], refs[10], refs[11]
    begin, rows = loaded_ref.shape[0] // 2, rest.shape[0] // 2
    copies = []
    for start in range(0, rows, begin):
        for side, ref in enumerate((top_ref, bottom_ref)):
            copies.append(pltpu.make_async_copy(
                ref.at[pl.ds(begin + start, begin)], rest.at[pl.ds(side * rows + start, begin)], sems.at[len(copies)]
            ))
            copies[-1].start()
    add_rows(accs, loaded_ref[:begin], loaded_ref[begin:], True)
    for idx, start in enumerate(range(0, rows, begin)):
        copies[2 * idx].wait()
        copies[2 * idx + 1].wait()
        add_rows(accs, rest[start:start + begin], rest[rows + start:rows + start + begin], False)
    put_pieces(accs, pieces, outs, where_ref[0])


def first_gram(where, own_a, top, bottom):
    rest = 2 * top.shape[0] - own_a.shape[0]
    return pl.pallas_call(
        first_gram_kernel,
        out_shape=[jax.ShapeDtypeStruct((PIECE, H), F32)] * 4 + [jax.ShapeDtypeStruct((rest, W), F32)],
        in_specs=[IN_SMEM, IN_VMEM, IN_HBM, IN_HBM],
        out_specs=[IN_VMEM] * 5,
        scratch_shapes=ACCS + [PIECES, pltpu.SemaphoreType.DMA((2 * rest // own_a.shape[0],))],
        compiler_params=granted(51),
        cost_estimate=pl.CostEstimate(flops=7 * 2 * W * W * 2048, bytes_accessed=2 ** 22, transcendentals=0),
    )(where, own_a, top, bottom)


def add_cross(cross, squares, top, bottom, begin):
    th, tl = split2(top)
    bh, bl = split2(bottom)
    share = dot_tn(th, bh) + (dot_tn(th, bl) + dot_tn(tl, bh))
    cross[...] = share if begin else cross[...] + share
    for idx, block in enumerate((top, bottom)):
        share = jnp.sum(block * block, axis=0, keepdims=True)
        squares[idx:idx + 1] = share if begin else squares[idx:idx + 1] + share


def early_cross_kernel(top_ref, bottom_ref, cross, squares):
    squares[...] = jnp.zeros_like(squares)
    add_cross(cross, squares, top_ref[:RAW], bottom_ref[:RAW], True)


def early_cross(top, bottom):
    return pl.pallas_call(
        early_cross_kernel,
        out_shape=[jax.ShapeDtypeStruct((W, W), F32), jax.ShapeDtypeStruct((8, W), F32)],
        in_specs=[IN_VMEM, IN_VMEM],
        out_specs=[IN_VMEM] * 2,
        compiler_params=granted(12),
        cost_estimate=pl.CostEstimate(flops=3 * 2 * W * W * 1024, bytes_accessed=2 ** 21, transcendentals=0),
    )(top, bottom)


def late_cross_kernel(count, where_ref, top_ref, bottom_ref, cross_ref, squares_ref, *refs):
    refs = refs[count:]
    outs, ship, cross, squares, pieces, sems = refs[:4], refs[4], refs[5], refs[6], refs[7], refs[8]
    late = top_ref.shape[0]
    early, mid = bottom_ref.shape[0] - late, (ship.shape[0] + MORE) // 2
    copies = [
        pltpu.make_async_copy(top_ref.at[pl.ds(0, mid)], ship.at[pl.ds(0, mid)], sems.at[0]),
        pltpu.make_async_copy(
            bottom_ref.at[pl.ds(early + MORE, mid - MORE)], ship.at[pl.ds(mid, mid - MORE)], sems.at[1]
        ),
    ]
    for copy in copies:
        copy.start()
    cross[...] = cross_ref[...]
    squares[...] = squares_ref[...]
    add_cross(cross, squares, top_ref[...], bottom_ref[early:], False)
    for idx in range(4):
        pieces[idx, :Q] = cross[idx * Q:(idx + 1) * Q]
        pieces[idx, Q:] = squares[...] if idx == 0 else jnp.zeros_like(squares)
    for ahead in range(4):
        outs[ahead][...] = pieces[(where_ref[0] + ahead) % 4]
    for copy in copies:
        copy.wait()


def late_cross(where, top, bottom, before, mid, after):
    return pl.pallas_call(
        functools.partial(late_cross_kernel, len(after)),
        out_shape=[jax.ShapeDtypeStruct((CROSS, W), F32)] * 4 + [jax.ShapeDtypeStruct((2 * mid - MORE, W), F32)],
        in_specs=[IN_SMEM] + [IN_VMEM] * 4 + [ANYWHERE] * len(after),
        out_specs=[IN_VMEM] * 5,
        scratch_shapes=[
            pltpu.VMEM((W, W), F32), pltpu.VMEM((8, W), F32), pltpu.VMEM((4, CROSS, W), F32),
            pltpu.SemaphoreType.DMA((2,)),
        ],
        compiler_params=granted(12),
        cost_estimate=pl.CostEstimate(flops=3 * 2 * W * W * 1024, bytes_accessed=2 ** 21, transcendentals=0),
    )(where, top, bottom, *before, *after)


def split3(x):
    high = x.astype(BF)
    rest = x - high.astype(F32)
    mid = rest.astype(BF)
    return high, mid, (rest - mid.astype(F32)).astype(BF)


def mm6(left, right, dot):
    (a, b, c), (x, y, z) = left, right
    return dot(a, x) + ((dot(a, y) + dot(b, x)) + (dot(b, y) + (dot(a, z) + dot(c, x))))


def turned_gram_kernel(count, gram_ref, *refs):
    whole = split3(gram_ref[...])
    for ref, out in zip(refs[:count], refs[count:]):
        turn = split3(ref[...])
        out[...] = mm6(turn, split3(mm6(whole, turn, dot_nn)), dot_tn)


def turned_grams(gram, *turns):
    return pl.pallas_call(
        functools.partial(turned_gram_kernel, len(turns)),
        out_shape=[jax.ShapeDtypeStruct((W, W), F32)] * len(turns),
        in_specs=[IN_VMEM] * (1 + len(turns)),
        out_specs=[IN_VMEM] * len(turns),
        compiler_params=granted(16),
        cost_estimate=pl.CostEstimate(flops=6 * (2 * W) ** 3 * len(turns), bytes_accessed=2 ** 21, transcendentals=0),
    )(gram, *turns)


def turn_columns(gram, sq_line, sq_col):
    sq_line, sq_col = sq_line + 1e-06, sq_col + 1e-06
    corr = gram * (1.0 / jnp.sqrt(sq_col)) * (1.0 / jnp.sqrt(sq_line))
    generator = corr * ((sq_line - sq_col) / (sq_line + sq_col))
    frobenius = jnp.sqrt(jnp.sum(generator * generator))
    skew = generator * (1.0 / (1.0 + frobenius))

    s2 = split2(skew)
    n = -mm3(s2, s2)
    n_2 = split2(n)
    nn = mm3(n_2, n_2)
    d1 = 0.25 * mm1(split2(nn), n_2) - 0.75 * nn
    d1_2 = split2(d1)
    dd = mm1(d1_2, d1_2)
    d2 = 0.25 * mm1(split2(dd), d1_2) - 0.75 * dd
    x = 0.5 * (d1 + d2) - 0.25 * mm1(d1_2, split2(d2))
    y = 0.5 * n + x - 0.5 * mm1(n_2, split2(x))
    row, col = iotas((2 * W, 2 * W))
    return jnp.where(row == col, 1.0, skew) - (y + mm3(s2, split2(y)))


def rotation_kernel(where_ref, q0, q1, q2, q3, *refs):
    first_ref, second_ref, gram, pieces = refs[-4:]
    mine = where_ref[0]
    for behind, piece in enumerate((q0, q1, q2, q3)):
        pieces[(mine + 4 - behind) % 4] = piece[...]
    row, col = iotas((H, H))
    upper, diag = row <= col, row == col

    def put(i, j, block):
        gram[i * H:(i + 1) * H, j * H:(j + 1) * H] = block

    lines, columns = [], []
    for half in range(2):
        off = pieces[half, 0:H]
        both = pieces[half, H:2 * H]
        line = pieces[half, 2 * H:2 * H + 1]
        turned = both.T
        first = jnp.where(upper, both, turned)
        last = jnp.where(diag, line, jnp.where(upper, turned, both))
        a, b = 2 * half, 2 * half + 1
        put(a, b, off)
        put(b, a, off.T)
        put(a, a, first)
        put(b, b, last)
        for block in (first, last):
            on = jnp.where(diag, block, 0.0)
            lines.append(jnp.sum(on, axis=0, keepdims=True))
            columns.append(jnp.sum(on, axis=1, keepdims=True))
    for i in range(2):
        for j in range(2):
            block = pieces[2 + i, j * H:(j + 1) * H]
            put(i, 2 + j, block)
            put(2 + j, i, block.T)
    rotate = turn_columns(gram[...], jnp.concatenate(lines, axis=1), jnp.concatenate(columns, axis=0))
    first_ref[...] = rotate[:, :W]
    second_ref[...] = rotate[:, W:]


def rotation(where, quarters, after=()):
    half = jax.ShapeDtypeStruct((2 * W, W), F32)
    return pl.pallas_call(
        rotation_kernel,
        out_shape=[half, half, jax.ShapeDtypeStruct((2 * W, 2 * W), F32)],
        in_specs=[IN_SMEM] + [IN_VMEM] * 4 + [ANYWHERE] * len(after),
        out_specs=[IN_VMEM] * 3,
        scratch_shapes=[PIECES],
        compiler_params=granted(20),
        cost_estimate=pl.CostEstimate(flops=14 * 2 * (2 * W) ** 3, bytes_accessed=2 ** 21, transcendentals=0),
    )(where, *quarters, *after)


def second_rotation_kernel(where_ref, q0, q1, q2, q3, top_ref, bottom_ref, first_ref, second_ref, pieces, gram):
    mine = where_ref[0]
    for behind, piece in enumerate((q0, q1, q2, q3)):
        pieces[(mine + 4 - behind) % 4] = piece[...]
    for idx in range(4):
        rows = slice(idx * Q, (idx + 1) * Q)
        gram[rows, W:] = pieces[idx, :Q]
    gram[:W, :W] = top_ref[...]
    gram[W:, W:] = bottom_ref[...]
    gram[W:, :W] = gram[:W, W:].T
    row, col = iotas((W, W))
    lines, columns = [], []
    for idx in range(2):
        line = pieces[0, Q + idx:Q + idx + 1]
        lines.append(line)
        columns.append(jnp.sum(jnp.where(row == col, line, 0.0), axis=1, keepdims=True))
    rotate = turn_columns(gram[...], jnp.concatenate(lines, axis=1), jnp.concatenate(columns, axis=0))
    first_ref[...] = rotate[:, :W]
    second_ref[...] = rotate[:, W:]


def second_rotation(where, quarters, top_gram, bottom_gram):
    half = jax.ShapeDtypeStruct((2 * W, W), F32)
    return pl.pallas_call(
        second_rotation_kernel,
        out_shape=[half, half],
        in_specs=[IN_SMEM] + [IN_VMEM] * 6,
        out_specs=[IN_VMEM] * 2,
        scratch_shapes=[pltpu.VMEM((4, CROSS, W), F32), pltpu.VMEM((2 * W, 2 * W), F32)],
        compiler_params=granted(20),
        cost_estimate=pl.CostEstimate(flops=14 * 2 * (2 * W) ** 3, bytes_accessed=2 ** 21, transcendentals=0),
    )(where, *quarters, top_gram, bottom_gram)


def apply_kernel(jobs, moves, n_in, n_turn, n_after, to_hbm, *refs):
    refs = refs[:n_in + n_turn] + refs[n_in + n_turn + n_after:]
    blocks, turns = refs[:n_in], [split2(ref[:2 * W]) for ref in refs[n_in:n_in + n_turn]]
    outs, scratch = refs[n_in + n_turn:n_in + n_turn + len(to_hbm)], refs[n_in + n_turn + len(to_hbm):]
    held, copies = list(outs), []
    for idx, hbm in enumerate(to_hbm):
        if hbm:
            held[idx] = scratch[2 * sum(to_hbm[:idx])]
    for top, top_start, bottom, bottom_start, rows, turn, places in jobs:
        high, low = turns[turn]
        for begin in range(0, rows, BLOCK):
            first = split2(blocks[top][top_start + begin:top_start + begin + BLOCK])
            second = split2(blocks[bottom][bottom_start + begin:bottom_start + begin + BLOCK])
            block = mm3(first, (high[:W], low[:W])) + mm3(second, (high[W:], low[W:]))
            for out, start in places:
                at = start + begin
                held[out][at:at + BLOCK] = block
                if to_hbm[out]:
                    span, sems = pl.ds(at, BLOCK), scratch[2 * sum(to_hbm[:out]) + 1]
                    copies.append(
                        pltpu.make_async_copy(held[out].at[span], outs[out].at[span], sems.at[at // BLOCK])
                    )
                    copies[-1].start()
    for source, start, rows, out, out_start in moves:
        held[out][out_start:out_start + rows] = refs[source][start:start + rows]
    for copy in copies:
        copy.wait()


def rotated(jobs, outs, moves=(), after=()):
    arrays, turns = [], []

    def index(array, known):
        for idx, other in enumerate(known):
            if other is array:
                return idx
        known.append(array)
        return len(known) - 1

    listed, count = [], 0
    for top, top_start, bottom, bottom_start, rows, turn, places in jobs:
        count += rows
        listed.append((index(top, arrays), top_start, index(bottom, arrays), bottom_start, rows, index(turn, turns),
                       tuple(places)))
    copied = [(index(array, arrays), start, rows, out, row) for array, start, rows, out, row in moves]
    scratch = []
    for rows, hbm in outs:
        if hbm:
            scratch += [pltpu.VMEM((rows, W), F32), pltpu.SemaphoreType.DMA((rows // BLOCK,))]
    result = pl.pallas_call(
        functools.partial(apply_kernel, listed, copied, len(arrays), len(turns), len(after), [hbm for _, hbm in outs]),
        out_shape=[jax.ShapeDtypeStruct((rows, W), F32) for rows, _ in outs],
        in_specs=[IN_VMEM] * (len(arrays) + len(turns)) + [ANYWHERE] * len(after),
        out_specs=[IN_HBM if hbm else IN_VMEM for _, hbm in outs],
        scratch_shapes=scratch,
        compiler_params=granted(12),
        cost_estimate=pl.CostEstimate(flops=6 * 2 * W * W * count, bytes_accessed=12 * W * count, transcendentals=0),
    )(*arrays, *turns, *after)
    return result


def sum_kernel(count, *refs):
    refs[-1][...] = functools.reduce(lambda a, b: a + b, [ref[...] for ref in refs[:count]])


def summed(terms, after):
    return pl.pallas_call(
        functools.partial(sum_kernel, len(terms)),
        out_shape=jax.ShapeDtypeStruct(terms[0].shape, F32),
        in_specs=[IN_VMEM] * len(terms) + [ANYWHERE] * len(after),
        out_specs=IN_VMEM,
        compiler_params=granted(2),
    )(*terms, *after)


def tie_kernel(*refs):
    pass


def tied(array, after):
    return pl.pallas_call(
        tie_kernel,
        out_shape=jax.ShapeDtypeStruct(array.shape, F32),
        in_specs=[ANYWHERE] * (1 + len(after)),
        out_specs=ANYWHERE,
        input_output_aliases={0: 0},
        compiler_params=granted(1),
    )(array, *after)


def last_kernel(count, *refs):
    parts, out_ref, sems = refs[:count], refs[count + 1], refs[count + 2]
    at, copies = out_ref.shape[0], []
    for idx in reversed(range(count)):
        rows = parts[idx].shape[0]
        at -= rows
        copies.append(pltpu.make_async_copy(parts[idx], out_ref.at[pl.ds(at, rows)], sems.at[idx]))
        copies[-1].start()
    for copy in copies:
        copy.wait()


def with_last(whole, parts):
    return pl.pallas_call(
        functools.partial(last_kernel, len(parts)),
        out_shape=jax.ShapeDtypeStruct(whole.shape, F32),
        in_specs=[IN_VMEM] * len(parts) + [IN_HBM],
        out_specs=IN_HBM,
        scratch_shapes=[pltpu.SemaphoreType.DMA((len(parts),))],
        input_output_aliases={len(parts): 0},
        compiler_params=granted(2),
    )(*parts, whole)


def passed_along(array, by=1):
    length = lax.axis_size("pair")
    return lax.ppermute(array, "pair", [(i, (i + by) % length) for i in range(length)])


def along_y(array, by):
    length = lax.axis_size("row") // 2
    return lax.ppermute(
        array, "row", [(2 * y + h, 2 * ((y + by) % length) + h) for y in range(length) for h in range(2)]
    )


def across_x(array):
    return lax.ppermute(array, "row", [(i, i ^ 1) for i in range(lax.axis_size("row"))])


def scattered(pieces, after):
    return summed([pieces[0]] + [along_y(pieces[r], r) for r in (1, 2, 3)], after)


def gathered_quarters(total):
    return [total] + [along_y(total, r) for r in (1, 2, 3)]


def on_device(top, bottom):
    where = (lax.axis_index("row") // 2).astype(jnp.int32).reshape(1)
    rows = top.shape[0]
    late = rows - RAW
    mid = late - LAST

    own_a = loaded(top, bottom, RAW)
    raw = passed_along(own_a)
    *pieces, own_b = first_gram(where, own_a, top, bottom)
    total = scattered(pieces, [raw])
    total = total + across_x(total)
    total_prev = passed_along(total)
    first, second, whole = rotation(where, gathered_quarters(total))
    (sent,) = rotated([(own_b, 0, own_b, late, late, first, [(0, 0)])], [(late, False)], after=[total_prev])
    quarters_prev = gathered_quarters(tied(total_prev, [sent]))
    sent = passed_along(sent)
    (bottom,) = rotated(
        [(own_a, 0, own_a, RAW, RAW, second, [(0, 0)]), (own_b, 0, own_b, late, late, second, [(0, RAW)])],
        [(rows, False)],
    )
    (bottom_gram,) = turned_grams(whole, second)
    first_prev, second_prev, whole_prev = rotation(where, quarters_prev, [bottom_gram])
    (early,) = rotated(
        [(raw, 0, raw, RAW, RAW, first_prev, [(0, 0)])], [(RAW + MORE, False)], [(bottom, RAW, MORE, 0, RAW)]
    )
    early_prev = passed_along(early)
    (top_gram,) = turned_grams(whole_prev, first_prev)

    *pieces, ship = late_cross(
        where, sent, bottom, early_cross(early, bottom), mid, []
    )
    total = scattered(pieces, [early_prev, top_gram])
    total = total + across_x(total)
    ship = passed_along(tied(ship, [total]))
    (bottom_prev,) = rotated([(raw, 0, raw, RAW, RAW, second_prev, [(0, 0)])], [(RAW, False)])
    first, second = second_rotation(where, gathered_quarters(total), top_gram, bottom_gram)
    first_prev = passed_along(first)
    *out_late, bottom_out = rotated(
        [
            (sent, mid, bottom, RAW + mid, LAST - W, first, [(0, 0)]),
            (sent, late - W, bottom, rows - W, W, first, [(1, 0)]),
            (early, 0, bottom, 0, RAW, second, [(2, 0)]),
            (sent, 0, bottom, RAW, late, second, [(2, RAW)]),
        ],
        [(LAST - W, False), (W, False), (rows, True)],
    )
    out_late = [passed_along(part) for part in out_late]
    (top_out,) = rotated(
        [
            (early_prev, 0, bottom_prev, 0, RAW, first_prev, [(0, 0)]),
            (ship, 0, early_prev, RAW, MORE, first_prev, [(0, RAW)]),
            (ship, MORE, ship, mid, mid - MORE, first_prev, [(0, RAW + MORE)]),
        ],
        [(rows, True)],
    )
    return (with_last(top_out, out_late), bottom_out)


def solution(mesh):
    placed = (P("row", "pair"), P("row", "pair"))
    return jax.shard_map(on_device, mesh=mesh, in_specs=placed, out_specs=placed, check_vma=False)
```

```python
import functools

import jax
import jax.numpy as jnp
from jax import lax
from jax.experimental import pallas as pl
from jax.experimental.pallas import tpu as pltpu
from jax.sharding import PartitionSpec as P

STEPS = 2
SWEEPS = 3
W = 256
H = 128
PIECE = 2 * H + 8
Q = W // 4
CROSS = Q + 8
RAW = 512
MORE = 256
LAST = 768
BLOCK = 256
BF, F32 = jnp.bfloat16, jnp.float32
IN_VMEM = pl.BlockSpec(memory_space=pltpu.VMEM)
IN_SMEM = pl.BlockSpec(memory_space=pltpu.SMEM)
IN_HBM = pl.BlockSpec(memory_space=pltpu.HBM)
ANYWHERE = pl.BlockSpec(memory_space=pl.ANY)
MIB = 1024 * 1024


def granted(mib):
    return pltpu.CompilerParams(vmem_limit_bytes=mib * MIB)


def split2(x):
    high = x.astype(BF)
    return high, (x - high.astype(F32)).astype(BF)


def dot_tn(left, right):
    return lax.dot_general(left, right, (((0,), (0,)), ((), ())), preferred_element_type=F32)


def dot_nn(left, right):
    return jnp.dot(left, right, preferred_element_type=F32)


def mm3(left, right, dot=dot_nn):
    lh, ll = left
    rh, rl = right
    return dot(lh, rh) + (dot(lh, rl) + dot(ll, rh))


def mm1(left, right):
    return dot_nn(left[0], right[0])


def iotas(shape):
    return lax.broadcasted_iota(jnp.int32, shape, 0), lax.broadcasted_iota(jnp.int32, shape, 1)


def add_rows(accs, top, bottom, begin):
    th, tl = split2(top)
    bh, bl = split2(bottom)
    shares = (
        dot_tn(th, th),
        dot_tn(th, tl),
        dot_tn(bh, bh),
        dot_tn(bh, bl),
        dot_tn(th, bh) + (dot_tn(th, bl) + dot_tn(tl, bh)),
    )
    for acc, share in zip(accs, shares):
        acc[...] = share if begin else acc[...] + share


def put_pieces(accs, pieces, outs, mine):
    xtt, ytt, xbb, ybb, tb = accs
    row, col = iotas((H, H))
    upper, diag = row <= col, row == col
    for idx, (x, y) in enumerate(((xtt, ytt), (xbb, ybb))):
        full = x[...] + (y[...] + y[...].T)
        first, last = full[:H, :H], full[H:, H:]
        pieces[idx, 0:H] = full[:H, H:]
        pieces[idx, H:2 * H] = jnp.where(upper, first, last)
        line = jnp.sum(jnp.where(diag, last, 0.0), axis=0, keepdims=True)
        pieces[idx, 2 * H:PIECE] = jnp.broadcast_to(line, (8, H))
    for idx in range(2):
        half = tb[idx * H:(idx + 1) * H, :]
        pieces[2 + idx, 0:H] = half[:, :H]
        pieces[2 + idx, H:2 * H] = half[:, H:]
        pieces[2 + idx, 2 * H:PIECE] = jnp.zeros((8, H), F32)
    for ahead in range(4):
        outs[ahead][...] = pieces[(mine + ahead) % 4]


ACCS = [pltpu.VMEM((W, W), F32)] * 5
PIECES = pltpu.VMEM((4, PIECE, H), F32)


def load_kernel(top_ref, bottom_ref, out_ref, sems):
    rows = out_ref.shape[0] // 2
    copies = [
        pltpu.make_async_copy(ref.at[pl.ds(0, rows)], out_ref.at[pl.ds(side * rows, rows)], sems.at[side])
        for side, ref in enumerate((top_ref, bottom_ref))
    ]
    for copy in copies:
        copy.start()
    for copy in copies:
        copy.wait()


def loaded(top, bottom, rows):
    return pl.pallas_call(
        load_kernel,
        out_shape=jax.ShapeDtypeStruct((2 * rows, W), F32),
        in_specs=[IN_HBM, IN_HBM],
        out_specs=IN_VMEM,
        scratch_shapes=[pltpu.SemaphoreType.DMA((2,))],
        compiler_params=granted(51),
        cost_estimate=pl.CostEstimate(flops=0, bytes_accessed=16 * W * rows, transcendentals=0),
    )(top, bottom)


def first_gram_kernel(where_ref, loaded_ref, top_ref, bottom_ref, *refs):
    outs, rest, accs, pieces, sems = refs[:4], refs[4], refs[5:10], refs[10], refs[11]
    begin, rows = loaded_ref.shape[0] // 2, rest.shape[0] // 2
    copies, size = [], rows // 2
    for start in range(0, rows, size):
        for side, ref in enumerate((top_ref, bottom_ref)):
            copies.append(pltpu.make_async_copy(
                ref.at[pl.ds(begin + start, size)], rest.at[pl.ds(side * rows + start, size)], sems.at[len(copies)]
            ))
            copies[-1].start()
    add_rows(accs, loaded_ref[:begin], loaded_ref[begin:], True)
    for idx, start in enumerate(range(0, rows, size)):
        copies[2 * idx].wait()
        copies[2 * idx + 1].wait()
        add_rows(accs, rest[start:start + size], rest[rows + start:rows + start + size], False)
    put_pieces(accs, pieces, outs, where_ref[0])


def first_gram(where, own_a, top, bottom):
    rest = 2 * top.shape[0] - own_a.shape[0]
    return pl.pallas_call(
        first_gram_kernel,
        out_shape=[jax.ShapeDtypeStruct((PIECE, H), F32)] * 4 + [jax.ShapeDtypeStruct((rest, W), F32)],
        in_specs=[IN_SMEM, IN_VMEM, IN_HBM, IN_HBM],
        out_specs=[IN_VMEM] * 5,
        scratch_shapes=ACCS + [PIECES, pltpu.SemaphoreType.DMA((2 * rest // own_a.shape[0],))],
        compiler_params=granted(51),
        cost_estimate=pl.CostEstimate(flops=7 * 2 * W * W * 2048, bytes_accessed=2 ** 22, transcendentals=0),
    )(where, own_a, top, bottom)


def add_cross(cross, squares, top, bottom, begin):
    th, tl = split2(top)
    bh, bl = split2(bottom)
    share = dot_tn(th, bh) + (dot_tn(th, bl) + dot_tn(tl, bh))
    cross[...] = share if begin else cross[...] + share
    for idx, block in enumerate((top, bottom)):
        share = jnp.sum(block * block, axis=0, keepdims=True)
        squares[idx:idx + 1] = share if begin else squares[idx:idx + 1] + share


def early_cross_kernel(top_ref, bottom_ref, cross, squares):
    squares[...] = jnp.zeros_like(squares)
    add_cross(cross, squares, top_ref[:RAW], bottom_ref[:RAW], True)


def early_cross(top, bottom):
    return pl.pallas_call(
        early_cross_kernel,
        out_shape=[jax.ShapeDtypeStruct((W, W), F32), jax.ShapeDtypeStruct((8, W), F32)],
        in_specs=[IN_VMEM, IN_VMEM],
        out_specs=[IN_VMEM] * 2,
        compiler_params=granted(12),
        cost_estimate=pl.CostEstimate(flops=3 * 2 * W * W * 1024, bytes_accessed=2 ** 21, transcendentals=0),
    )(top, bottom)


def late_cross_kernel(count, where_ref, top_ref, bottom_ref, cross_ref, squares_ref, *refs):
    refs = refs[count:]
    outs, ship, cross, squares, pieces, sems = refs[:4], refs[4], refs[5], refs[6], refs[7], refs[8]
    late = top_ref.shape[0]
    early, mid = bottom_ref.shape[0] - late, (ship.shape[0] + MORE) // 2
    copies = [
        pltpu.make_async_copy(top_ref.at[pl.ds(0, mid)], ship.at[pl.ds(0, mid)], sems.at[0]),
        pltpu.make_async_copy(
            bottom_ref.at[pl.ds(early + MORE, mid - MORE)], ship.at[pl.ds(mid, mid - MORE)], sems.at[1]
        ),
    ]
    for copy in copies:
        copy.start()
    cross[...] = cross_ref[...]
    squares[...] = squares_ref[...]
    add_cross(cross, squares, top_ref[...], bottom_ref[early:], False)
    for idx in range(4):
        pieces[idx, :Q] = cross[idx * Q:(idx + 1) * Q]
        pieces[idx, Q:] = squares[...] if idx == 0 else jnp.zeros_like(squares)
    for ahead in range(4):
        outs[ahead][...] = pieces[(where_ref[0] + ahead) % 4]
    for copy in copies:
        copy.wait()


def late_cross(where, top, bottom, before, mid, after):
    return pl.pallas_call(
        functools.partial(late_cross_kernel, len(after)),
        out_shape=[jax.ShapeDtypeStruct((CROSS, W), F32)] * 4 + [jax.ShapeDtypeStruct((2 * mid - MORE, W), F32)],
        in_specs=[IN_SMEM] + [IN_VMEM] * 4 + [ANYWHERE] * len(after),
        out_specs=[IN_VMEM] * 5,
        scratch_shapes=[
            pltpu.VMEM((W, W), F32), pltpu.VMEM((8, W), F32), pltpu.VMEM((4, CROSS, W), F32),
            pltpu.SemaphoreType.DMA((2,)),
        ],
        compiler_params=granted(12),
        cost_estimate=pl.CostEstimate(flops=3 * 2 * W * W * 1024, bytes_accessed=2 ** 21, transcendentals=0),
    )(where, top, bottom, *before, *after)


def turned_gram_kernel(count, gram_ref, *refs):
    whole = split2(gram_ref[...])
    for ref, out in zip(refs[:count], refs[count:]):
        turn = split2(ref[...])
        out[...] = mm3(turn, split2(mm3(whole, turn)), dot_tn)


def turned_grams(gram, *turns):
    return pl.pallas_call(
        functools.partial(turned_gram_kernel, len(turns)),
        out_shape=[jax.ShapeDtypeStruct((W, W), F32)] * len(turns),
        in_specs=[IN_VMEM] * (1 + len(turns)),
        out_specs=[IN_VMEM] * len(turns),
        compiler_params=granted(16),
        cost_estimate=pl.CostEstimate(flops=3 * (2 * W) ** 3 * len(turns), bytes_accessed=2 ** 21, transcendentals=0),
    )(gram, *turns)


def turn_columns(gram, sq_line, sq_col):
    sq_line, sq_col = sq_line + 1e-06, sq_col + 1e-06
    corr = gram * (1.0 / jnp.sqrt(sq_col)) * (1.0 / jnp.sqrt(sq_line))
    generator = corr * ((sq_line - sq_col) / (sq_line + sq_col))
    frobenius = jnp.sqrt(jnp.sum(generator * generator))
    skew = generator * (1.0 / (1.0 + frobenius))

    s2 = split2(skew)
    n = -mm3(s2, s2)
    n_2 = split2(n)
    nn = mm3(n_2, n_2)
    d1 = 0.25 * mm1(split2(nn), n_2) - 0.75 * nn
    d1_2 = split2(d1)
    dd = mm1(d1_2, d1_2)
    d2 = 0.25 * mm1(split2(dd), d1_2) - 0.75 * dd
    x = 0.5 * (d1 + d2) - 0.25 * mm1(d1_2, split2(d2))
    y = 0.5 * n + x - 0.5 * mm1(n_2, split2(x))
    row, col = iotas((2 * W, 2 * W))
    return jnp.where(row == col, 1.0, skew) - (y + mm3(s2, split2(y)))


def rotation_kernel(where_ref, q0, q1, q2, q3, *refs):
    first_ref, second_ref, gram, pieces = refs[-4:]
    mine = where_ref[0]
    for behind, piece in enumerate((q0, q1, q2, q3)):
        pieces[(mine + 4 - behind) % 4] = piece[...]
    row, col = iotas((H, H))
    upper, diag = row <= col, row == col

    def put(i, j, block):
        gram[i * H:(i + 1) * H, j * H:(j + 1) * H] = block

    lines, columns = [], []
    for half in range(2):
        off = pieces[half, 0:H]
        both = pieces[half, H:2 * H]
        line = pieces[half, 2 * H:2 * H + 1]
        turned = both.T
        first = jnp.where(upper, both, turned)
        last = jnp.where(diag, line, jnp.where(upper, turned, both))
        a, b = 2 * half, 2 * half + 1
        put(a, b, off)
        put(b, a, off.T)
        put(a, a, first)
        put(b, b, last)
        for block in (first, last):
            on = jnp.where(diag, block, 0.0)
            lines.append(jnp.sum(on, axis=0, keepdims=True))
            columns.append(jnp.sum(on, axis=1, keepdims=True))
    for i in range(2):
        for j in range(2):
            block = pieces[2 + i, j * H:(j + 1) * H]
            put(i, 2 + j, block)
            put(2 + j, i, block.T)
    rotate = turn_columns(gram[...], jnp.concatenate(lines, axis=1), jnp.concatenate(columns, axis=0))
    first_ref[...] = rotate[:, :W]
    second_ref[...] = rotate[:, W:]


def rotation(where, quarters, after=()):
    half = jax.ShapeDtypeStruct((2 * W, W), F32)
    return pl.pallas_call(
        rotation_kernel,
        out_shape=[half, half, jax.ShapeDtypeStruct((2 * W, 2 * W), F32)],
        in_specs=[IN_SMEM] + [IN_VMEM] * 4 + [ANYWHERE] * len(after),
        out_specs=[IN_VMEM] * 3,
        scratch_shapes=[PIECES],
        compiler_params=granted(20),
        cost_estimate=pl.CostEstimate(flops=14 * 2 * (2 * W) ** 3, bytes_accessed=2 ** 21, transcendentals=0),
    )(where, *quarters, *after)


def second_rotation_kernel(where_ref, q0, q1, q2, q3, top_ref, bottom_ref, first_ref, second_ref, pieces, gram):
    mine = where_ref[0]
    for behind, piece in enumerate((q0, q1, q2, q3)):
        pieces[(mine + 4 - behind) % 4] = piece[...]
    for idx in range(4):
        rows = slice(idx * Q, (idx + 1) * Q)
        gram[rows, W:] = pieces[idx, :Q]
    gram[:W, :W] = top_ref[...]
    gram[W:, W:] = bottom_ref[...]
    gram[W:, :W] = gram[:W, W:].T
    row, col = iotas((W, W))
    lines, columns = [], []
    for idx in range(2):
        line = pieces[0, Q + idx:Q + idx + 1]
        lines.append(line)
        columns.append(jnp.sum(jnp.where(row == col, line, 0.0), axis=1, keepdims=True))
    rotate = turn_columns(gram[...], jnp.concatenate(lines, axis=1), jnp.concatenate(columns, axis=0))
    first_ref[...] = rotate[:, :W]
    second_ref[...] = rotate[:, W:]


def second_rotation(where, quarters, top_gram, bottom_gram):
    half = jax.ShapeDtypeStruct((2 * W, W), F32)
    return pl.pallas_call(
        second_rotation_kernel,
        out_shape=[half, half],
        in_specs=[IN_SMEM] + [IN_VMEM] * 6,
        out_specs=[IN_VMEM] * 2,
        scratch_shapes=[pltpu.VMEM((4, CROSS, W), F32), pltpu.VMEM((2 * W, 2 * W), F32)],
        compiler_params=granted(20),
        cost_estimate=pl.CostEstimate(flops=14 * 2 * (2 * W) ** 3, bytes_accessed=2 ** 21, transcendentals=0),
    )(where, *quarters, top_gram, bottom_gram)


def apply_kernel(jobs, moves, n_in, n_turn, n_after, to_hbm, *refs):
    refs = refs[:n_in + n_turn] + refs[n_in + n_turn + n_after:]
    blocks, turns = refs[:n_in], [split2(ref[:2 * W]) for ref in refs[n_in:n_in + n_turn]]
    outs, scratch = refs[n_in + n_turn:n_in + n_turn + len(to_hbm)], refs[n_in + n_turn + len(to_hbm):]
    held, copies = list(outs), []
    for idx, hbm in enumerate(to_hbm):
        if hbm:
            held[idx] = scratch[2 * sum(to_hbm[:idx])]
    for top, top_start, bottom, bottom_start, rows, turn, places in jobs:
        high, low = turns[turn]
        for begin in range(0, rows, BLOCK):
            first = split2(blocks[top][top_start + begin:top_start + begin + BLOCK])
            second = split2(blocks[bottom][bottom_start + begin:bottom_start + begin + BLOCK])
            block = mm3(first, (high[:W], low[:W])) + mm3(second, (high[W:], low[W:]))
            for out, start in places:
                at = start + begin
                held[out][at:at + BLOCK] = block
                if to_hbm[out]:
                    span, sems = pl.ds(at, BLOCK), scratch[2 * sum(to_hbm[:out]) + 1]
                    copies.append(
                        pltpu.make_async_copy(held[out].at[span], outs[out].at[span], sems.at[at // BLOCK])
                    )
                    copies[-1].start()
    for source, start, rows, out, out_start in moves:
        held[out][out_start:out_start + rows] = refs[source][start:start + rows]
    for copy in copies:
        copy.wait()


def rotated(jobs, outs, moves=(), after=()):
    arrays, turns = [], []

    def index(array, known):
        for idx, other in enumerate(known):
            if other is array:
                return idx
        known.append(array)
        return len(known) - 1

    listed, count = [], 0
    for top, top_start, bottom, bottom_start, rows, turn, places in jobs:
        count += rows
        listed.append((index(top, arrays), top_start, index(bottom, arrays), bottom_start, rows, index(turn, turns),
                       tuple(places)))
    copied = [(index(array, arrays), start, rows, out, row) for array, start, rows, out, row in moves]
    scratch = []
    for rows, hbm in outs:
        if hbm:
            scratch += [pltpu.VMEM((rows, W), F32), pltpu.SemaphoreType.DMA((rows // BLOCK,))]
    result = pl.pallas_call(
        functools.partial(apply_kernel, listed, copied, len(arrays), len(turns), len(after), [hbm for _, hbm in outs]),
        out_shape=[jax.ShapeDtypeStruct((rows, W), F32) for rows, _ in outs],
        in_specs=[IN_VMEM] * (len(arrays) + len(turns)) + [ANYWHERE] * len(after),
        out_specs=[IN_HBM if hbm else IN_VMEM for _, hbm in outs],
        scratch_shapes=scratch,
        compiler_params=granted(12),
        cost_estimate=pl.CostEstimate(flops=6 * 2 * W * W * count, bytes_accessed=12 * W * count, transcendentals=0),
    )(*arrays, *turns, *after)
    return result


def sum_kernel(count, *refs):
    refs[-1][...] = functools.reduce(lambda a, b: a + b, [ref[...] for ref in refs[:count]])


def summed(terms, after):
    return pl.pallas_call(
        functools.partial(sum_kernel, len(terms)),
        out_shape=jax.ShapeDtypeStruct(terms[0].shape, F32),
        in_specs=[IN_VMEM] * len(terms) + [ANYWHERE] * len(after),
        out_specs=IN_VMEM,
        compiler_params=granted(2),
    )(*terms, *after)


def tie_kernel(*refs):
    pass


def tied(array, after):
    return pl.pallas_call(
        tie_kernel,
        out_shape=jax.ShapeDtypeStruct(array.shape, F32),
        in_specs=[ANYWHERE] * (1 + len(after)),
        out_specs=ANYWHERE,
        input_output_aliases={0: 0},
        compiler_params=granted(1),
    )(array, *after)


def last_kernel(count, *refs):
    parts, out_ref, sems = refs[:count], refs[count + 1], refs[count + 2]
    at, copies = out_ref.shape[0], []
    for idx in reversed(range(count)):
        rows = parts[idx].shape[0]
        at -= rows
        copies.append(pltpu.make_async_copy(parts[idx], out_ref.at[pl.ds(at, rows)], sems.at[idx]))
        copies[-1].start()
    for copy in copies:
        copy.wait()


def with_last(whole, parts):
    return pl.pallas_call(
        functools.partial(last_kernel, len(parts)),
        out_shape=jax.ShapeDtypeStruct(whole.shape, F32),
        in_specs=[IN_VMEM] * len(parts) + [IN_HBM],
        out_specs=IN_HBM,
        scratch_shapes=[pltpu.SemaphoreType.DMA((len(parts),))],
        input_output_aliases={len(parts): 0},
        compiler_params=granted(2),
    )(*parts, whole)


def passed_along(array, by=1):
    length = lax.axis_size("pair")
    return lax.ppermute(array, "pair", [(i, (i + by) % length) for i in range(length)])


def along_y(array, by):
    length = lax.axis_size("row") // 2
    return lax.ppermute(
        array, "row", [(2 * y + h, 2 * ((y + by) % length) + h) for y in range(length) for h in range(2)]
    )


def across_x(array):
    return lax.ppermute(array, "row", [(i, i ^ 1) for i in range(lax.axis_size("row"))])


def scattered(pieces, after):
    return summed([pieces[0]] + [along_y(pieces[r], r) for r in (1, 2, 3)], after)


def gathered_quarters(total):
    return [total] + [along_y(total, r) for r in (1, 2, 3)]


def on_device(top, bottom):
    where = (lax.axis_index("row") // 2).astype(jnp.int32).reshape(1)
    rows = top.shape[0]
    late = rows - RAW
    mid = late - LAST

    own_a = loaded(top, bottom, RAW)
    raw = passed_along(own_a)
    *pieces, own_b = first_gram(where, own_a, top, bottom)
    total = scattered(pieces, [])
    total = summed([total, across_x(total)], [raw])
    total_prev = passed_along(total)
    first, second, whole = rotation(where, gathered_quarters(total))
    (sent,) = rotated([(own_b, 0, own_b, late, late, first, [(0, 0)])], [(late, False)], after=[total_prev])
    quarters_prev = gathered_quarters(tied(total_prev, [sent]))
    sent = passed_along(sent)
    (bottom,) = rotated(
        [(own_a, 0, own_a, RAW, RAW, second, [(0, 0)]), (own_b, 0, own_b, late, late, second, [(0, RAW)])],
        [(rows, False)],
    )
    (bottom_gram,) = turned_grams(whole, second)
    first_prev, second_prev, whole_prev = rotation(where, quarters_prev, [bottom_gram])
    (early,) = rotated(
        [(raw, 0, raw, RAW, RAW, first_prev, [(0, 0)])], [(RAW + MORE, False)], [(bottom, RAW, MORE, 0, RAW)]
    )
    early_prev = passed_along(early)
    (top_gram,) = turned_grams(whole_prev, first_prev)

    *pieces, ship = late_cross(
        where, sent, bottom, early_cross(early, bottom), mid, []
    )
    total = scattered(pieces, [early_prev, top_gram])
    total = total + across_x(total)
    ship = passed_along(tied(ship, [total]))
    (bottom_prev,) = rotated([(raw, 0, raw, RAW, RAW, second_prev, [(0, 0)])], [(RAW, False)])
    first, second = second_rotation(where, gathered_quarters(total), top_gram, bottom_gram)
    first_prev = passed_along(first)
    *out_late, bottom_out = rotated(
        [
            (sent, mid, bottom, RAW + mid, LAST - W, first, [(0, 0)]),
            (sent, late - W, bottom, rows - W, W, first, [(1, 0)]),
            (early, 0, bottom, 0, RAW, second, [(2, 0)]),
            (sent, 0, bottom, RAW, late, second, [(2, RAW)]),
        ],
        [(LAST - W, False), (W, False), (rows, True)],
    )
    out_late = [passed_along(part) for part in out_late]
    (top_out,) = rotated(
        [
            (early_prev, 0, bottom_prev, 0, RAW, first_prev, [(0, 0)]),
            (ship, 0, early_prev, RAW, MORE, first_prev, [(0, RAW)]),
            (ship, MORE, ship, mid, mid - MORE, first_prev, [(0, RAW + MORE)]),
        ],
        [(rows, True)],
    )
    return (with_last(top_out, out_late), bottom_out)


def solution(mesh):
    placed = (P("row", "pair"), P("row", "pair"))
    return jax.shard_map(on_device, mesh=mesh, in_specs=placed, out_specs=placed, check_vma=False)
```

```python
import functools

import jax
import jax.numpy as jnp
from jax import lax
from jax.experimental import pallas as pl
from jax.experimental.pallas import tpu as pltpu
from jax.sharding import PartitionSpec as P

STEPS = 2
SWEEPS = 3
W = 256
H = 128
PIECE = 2 * H + 8
Q = W // 4
CROSS = Q + 8
RAW = 512
MORE = 256
LAST = 768
BLOCK = 256
BF, F32 = jnp.bfloat16, jnp.float32
IN_VMEM = pl.BlockSpec(memory_space=pltpu.VMEM)
IN_SMEM = pl.BlockSpec(memory_space=pltpu.SMEM)
IN_HBM = pl.BlockSpec(memory_space=pltpu.HBM)
ANYWHERE = pl.BlockSpec(memory_space=pl.ANY)
MIB = 1024 * 1024


def granted(mib):
    return pltpu.CompilerParams(vmem_limit_bytes=mib * MIB)


def split2(x):
    high = x.astype(BF)
    return high, (x - high.astype(F32)).astype(BF)


def dot_tn(left, right):
    return lax.dot_general(left, right, (((0,), (0,)), ((), ())), preferred_element_type=F32)


def dot_nn(left, right):
    return jnp.dot(left, right, preferred_element_type=F32)


def mm3(left, right, dot=dot_nn):
    lh, ll = left
    rh, rl = right
    return dot(lh, rh) + (dot(lh, rl) + dot(ll, rh))


def mm1(left, right):
    return dot_nn(left[0], right[0])


def iotas(shape):
    return lax.broadcasted_iota(jnp.int32, shape, 0), lax.broadcasted_iota(jnp.int32, shape, 1)


def add_rows(accs, top, bottom, begin):
    th, tl = split2(top)
    bh, bl = split2(bottom)
    shares = (
        dot_tn(th, th),
        dot_tn(th, tl),
        dot_tn(bh, bh),
        dot_tn(bh, bl),
        dot_tn(th, bh) + (dot_tn(th, bl) + dot_tn(tl, bh)),
    )
    for acc, share in zip(accs, shares):
        acc[...] = share if begin else acc[...] + share


def put_pieces(accs, pieces, outs, mine):
    xtt, ytt, xbb, ybb, tb = accs
    row, col = iotas((H, H))
    upper, diag = row <= col, row == col
    for idx, (x, y) in enumerate(((xtt, ytt), (xbb, ybb))):
        full = x[...] + (y[...] + y[...].T)
        first, last = full[:H, :H], full[H:, H:]
        pieces[idx, 0:H] = full[:H, H:]
        pieces[idx, H:2 * H] = jnp.where(upper, first, last)
        line = jnp.sum(jnp.where(diag, last, 0.0), axis=0, keepdims=True)
        pieces[idx, 2 * H:PIECE] = jnp.broadcast_to(line, (8, H))
    for idx in range(2):
        half = tb[idx * H:(idx + 1) * H, :]
        pieces[2 + idx, 0:H] = half[:, :H]
        pieces[2 + idx, H:2 * H] = half[:, H:]
        pieces[2 + idx, 2 * H:PIECE] = jnp.zeros((8, H), F32)
    for ahead in range(4):
        outs[ahead][...] = pieces[(mine + ahead) % 4]


ACCS = [pltpu.VMEM((W, W), F32)] * 5
PIECES = pltpu.VMEM((4, PIECE, H), F32)


def load_kernel(top_ref, bottom_ref, out_ref, sems):
    rows = out_ref.shape[0] // 2
    copies = [
        pltpu.make_async_copy(ref.at[pl.ds(0, rows)], out_ref.at[pl.ds(side * rows, rows)], sems.at[side])
        for side, ref in enumerate((top_ref, bottom_ref))
    ]
    for copy in copies:
        copy.start()
    for copy in copies:
        copy.wait()


def loaded(top, bottom, rows):
    return pl.pallas_call(
        load_kernel,
        out_shape=jax.ShapeDtypeStruct((2 * rows, W), F32),
        in_specs=[IN_HBM, IN_HBM],
        out_specs=IN_VMEM,
        scratch_shapes=[pltpu.SemaphoreType.DMA((2,))],
        compiler_params=granted(51),
        cost_estimate=pl.CostEstimate(flops=0, bytes_accessed=16 * W * rows, transcendentals=0),
    )(top, bottom)


def first_gram_kernel(where_ref, loaded_ref, top_ref, bottom_ref, *refs):
    outs, rest, accs, pieces, sems = refs[:4], refs[4], refs[5:10], refs[10], refs[11]
    size, rows = loaded_ref.shape[0] // 2, rest.shape[0] // 2

    def copies(part):
        start = pl.multiple_of(part * size, size)
        return [
            pltpu.make_async_copy(
                ref.at[pl.ds(pl.multiple_of(start + size, size), size)],
                rest.at[pl.ds(pl.multiple_of(side * rows + start, size), size)],
                sems.at[2 * part + side],
            )
            for side, ref in enumerate((top_ref, bottom_ref))
        ]

    for part in range(rows // size):
        for copy in copies(part):
            copy.start()
    add_rows(accs, loaded_ref[:size], loaded_ref[size:], True)

    @pl.loop(0, rows // size)
    def _(part):
        for copy in copies(part):
            copy.wait()
        start = pl.multiple_of(part * size, size)
        add_rows(accs, rest[pl.ds(start, size)], rest[pl.ds(pl.multiple_of(rows + start, size), size)], False)

    put_pieces(accs, pieces, outs, where_ref[0])


def first_gram(where, own_a, top, bottom):
    rest = 2 * top.shape[0] - own_a.shape[0]
    return pl.pallas_call(
        first_gram_kernel,
        out_shape=[jax.ShapeDtypeStruct((PIECE, H), F32)] * 4 + [jax.ShapeDtypeStruct((rest, W), F32)],
        in_specs=[IN_SMEM, IN_VMEM, IN_HBM, IN_HBM],
        out_specs=[IN_VMEM] * 5,
        scratch_shapes=ACCS + [PIECES, pltpu.SemaphoreType.DMA((2 * rest // own_a.shape[0],))],
        compiler_params=granted(51),
        cost_estimate=pl.CostEstimate(flops=7 * 2 * W * W * 2048, bytes_accessed=2 ** 22, transcendentals=0),
    )(where, own_a, top, bottom)


def add_cross(cross, squares, top, bottom, begin):
    th, tl = split2(top)
    bh, bl = split2(bottom)
    share = dot_tn(th, bh) + (dot_tn(th, bl) + dot_tn(tl, bh))
    cross[...] = share if begin else cross[...] + share
    for idx, block in enumerate((top, bottom)):
        share = jnp.sum(block * block, axis=0, keepdims=True)
        squares[idx:idx + 1] = share if begin else squares[idx:idx + 1] + share


def early_cross_kernel(top_ref, bottom_ref, cross, squares):
    squares[...] = jnp.zeros_like(squares)
    add_cross(cross, squares, top_ref[:RAW], bottom_ref[:RAW], True)


def early_cross(top, bottom):
    return pl.pallas_call(
        early_cross_kernel,
        out_shape=[jax.ShapeDtypeStruct((W, W), F32), jax.ShapeDtypeStruct((8, W), F32)],
        in_specs=[IN_VMEM, IN_VMEM],
        out_specs=[IN_VMEM] * 2,
        compiler_params=granted(12),
        cost_estimate=pl.CostEstimate(flops=3 * 2 * W * W * 1024, bytes_accessed=2 ** 21, transcendentals=0),
    )(top, bottom)


def late_cross_kernel(count, where_ref, top_ref, bottom_ref, cross_ref, squares_ref, *refs):
    refs = refs[count:]
    outs, ship, cross, squares, pieces, sems = refs[:4], refs[4], refs[5], refs[6], refs[7], refs[8]
    late = top_ref.shape[0]
    early, mid = bottom_ref.shape[0] - late, (ship.shape[0] + MORE) // 2
    copies = [
        pltpu.make_async_copy(top_ref.at[pl.ds(0, mid)], ship.at[pl.ds(0, mid)], sems.at[0]),
        pltpu.make_async_copy(
            bottom_ref.at[pl.ds(early + MORE, mid - MORE)], ship.at[pl.ds(mid, mid - MORE)], sems.at[1]
        ),
    ]
    for copy in copies:
        copy.start()
    cross[...] = cross_ref[...]
    squares[...] = squares_ref[...]

    @pl.loop(0, top_ref.shape[0] // 512)
    def _(step):
        begin = pl.multiple_of(step * 512, 512)
        add_cross(cross, squares, top_ref[pl.ds(begin, 512)], bottom_ref[pl.ds(early + begin, 512)], False)

    for idx in range(4):
        pieces[idx, :Q] = cross[idx * Q:(idx + 1) * Q]
        pieces[idx, Q:] = squares[...] if idx == 0 else jnp.zeros_like(squares)
    for ahead in range(4):
        outs[ahead][...] = pieces[(where_ref[0] + ahead) % 4]
    for copy in copies:
        copy.wait()


def late_cross(where, top, bottom, before, mid, after):
    return pl.pallas_call(
        functools.partial(late_cross_kernel, len(after)),
        out_shape=[jax.ShapeDtypeStruct((CROSS, W), F32)] * 4 + [jax.ShapeDtypeStruct((2 * mid - MORE, W), F32)],
        in_specs=[IN_SMEM] + [IN_VMEM] * 4 + [ANYWHERE] * len(after),
        out_specs=[IN_VMEM] * 5,
        scratch_shapes=[
            pltpu.VMEM((W, W), F32), pltpu.VMEM((8, W), F32), pltpu.VMEM((4, CROSS, W), F32),
            pltpu.SemaphoreType.DMA((2,)),
        ],
        compiler_params=granted(12),
        cost_estimate=pl.CostEstimate(flops=3 * 2 * W * W * 1024, bytes_accessed=2 ** 21, transcendentals=0),
    )(where, top, bottom, *before, *after)


def turned_gram_kernel(count, gram_ref, *refs):
    whole = split2(gram_ref[...])
    for ref, out in zip(refs[:count], refs[count:]):
        turn = split2(ref[...])
        out[...] = mm3(turn, split2(mm3(whole, turn)), dot_tn)


def turned_grams(gram, *turns):
    return pl.pallas_call(
        functools.partial(turned_gram_kernel, len(turns)),
        out_shape=[jax.ShapeDtypeStruct((W, W), F32)] * len(turns),
        in_specs=[IN_VMEM] * (1 + len(turns)),
        out_specs=[IN_VMEM] * len(turns),
        compiler_params=granted(16),
        cost_estimate=pl.CostEstimate(flops=3 * (2 * W) ** 3 * len(turns), bytes_accessed=2 ** 21, transcendentals=0),
    )(gram, *turns)


def turn_columns(gram, sq_line, sq_col):
    sq_line, sq_col = sq_line + 1e-06, sq_col + 1e-06
    corr = gram * (1.0 / jnp.sqrt(sq_col)) * (1.0 / jnp.sqrt(sq_line))
    generator = corr * ((sq_line - sq_col) / (sq_line + sq_col))
    frobenius = jnp.sqrt(jnp.sum(generator * generator))
    skew = generator * (1.0 / (1.0 + frobenius))

    s2 = split2(skew)
    n = -mm3(s2, s2)
    n_2 = split2(n)
    nn = mm3(n_2, n_2)
    d1 = 0.25 * mm1(split2(nn), n_2) - 0.75 * nn
    d1_2 = split2(d1)
    dd = mm1(d1_2, d1_2)
    d2 = 0.25 * mm1(split2(dd), d1_2) - 0.75 * dd
    x = 0.5 * (d1 + d2) - 0.25 * mm1(d1_2, split2(d2))
    y = 0.5 * n + x - 0.5 * mm1(n_2, split2(x))
    row, col = iotas((2 * W, 2 * W))
    return jnp.where(row == col, 1.0, skew) - (y + mm3(s2, split2(y)))


def rotation_kernel(where_ref, q0, q1, q2, q3, *refs):
    first_ref, second_ref, gram, pieces = refs[-4:]
    mine = where_ref[0]
    for behind, piece in enumerate((q0, q1, q2, q3)):
        pieces[(mine + 4 - behind) % 4] = piece[...]
    row, col = iotas((H, H))
    upper, diag = row <= col, row == col

    def put(i, j, block):
        gram[i * H:(i + 1) * H, j * H:(j + 1) * H] = block

    lines, columns = [], []
    for half in range(2):
        off = pieces[half, 0:H]
        both = pieces[half, H:2 * H]
        line = pieces[half, 2 * H:2 * H + 1]
        turned = both.T
        first = jnp.where(upper, both, turned)
        last = jnp.where(diag, line, jnp.where(upper, turned, both))
        a, b = 2 * half, 2 * half + 1
        put(a, b, off)
        put(b, a, off.T)
        put(a, a, first)
        put(b, b, last)
        for block in (first, last):
            on = jnp.where(diag, block, 0.0)
            lines.append(jnp.sum(on, axis=0, keepdims=True))
            columns.append(jnp.sum(on, axis=1, keepdims=True))
    for i in range(2):
        for j in range(2):
            block = pieces[2 + i, j * H:(j + 1) * H]
            put(i, 2 + j, block)
            put(2 + j, i, block.T)
    rotate = turn_columns(gram[...], jnp.concatenate(lines, axis=1), jnp.concatenate(columns, axis=0))
    first_ref[...] = rotate[:, :W]
    second_ref[...] = rotate[:, W:]


def rotation(where, quarters, after=()):
    half = jax.ShapeDtypeStruct((2 * W, W), F32)
    return pl.pallas_call(
        rotation_kernel,
        out_shape=[half, half, jax.ShapeDtypeStruct((2 * W, 2 * W), F32)],
        in_specs=[IN_SMEM] + [IN_VMEM] * 4 + [ANYWHERE] * len(after),
        out_specs=[IN_VMEM] * 3,
        scratch_shapes=[PIECES],
        compiler_params=granted(20),
        cost_estimate=pl.CostEstimate(flops=14 * 2 * (2 * W) ** 3, bytes_accessed=2 ** 21, transcendentals=0),
    )(where, *quarters, *after)


def second_rotation_kernel(where_ref, q0, q1, q2, q3, top_ref, bottom_ref, first_ref, second_ref, pieces, gram):
    mine = where_ref[0]
    for behind, piece in enumerate((q0, q1, q2, q3)):
        pieces[(mine + 4 - behind) % 4] = piece[...]
    for idx in range(4):
        rows = slice(idx * Q, (idx + 1) * Q)
        gram[rows, W:] = pieces[idx, :Q]
    gram[:W, :W] = top_ref[...]
    gram[W:, W:] = bottom_ref[...]
    gram[W:, :W] = gram[:W, W:].T
    row, col = iotas((W, W))
    lines, columns = [], []
    for idx in range(2):
        line = pieces[0, Q + idx:Q + idx + 1]
        lines.append(line)
        columns.append(jnp.sum(jnp.where(row == col, line, 0.0), axis=1, keepdims=True))
    rotate = turn_columns(gram[...], jnp.concatenate(lines, axis=1), jnp.concatenate(columns, axis=0))
    first_ref[...] = rotate[:, :W]
    second_ref[...] = rotate[:, W:]


def second_rotation(where, quarters, top_gram, bottom_gram):
    half = jax.ShapeDtypeStruct((2 * W, W), F32)
    return pl.pallas_call(
        second_rotation_kernel,
        out_shape=[half, half],
        in_specs=[IN_SMEM] + [IN_VMEM] * 6,
        out_specs=[IN_VMEM] * 2,
        scratch_shapes=[pltpu.VMEM((4, CROSS, W), F32), pltpu.VMEM((2 * W, 2 * W), F32)],
        compiler_params=granted(20),
        cost_estimate=pl.CostEstimate(flops=14 * 2 * (2 * W) ** 3, bytes_accessed=2 ** 21, transcendentals=0),
    )(where, *quarters, top_gram, bottom_gram)


def apply_kernel(jobs, moves, n_in, n_turn, n_after, to_hbm, rolled, *refs):
    refs = refs[:n_in + n_turn] + refs[n_in + n_turn + n_after:]
    blocks, turns = refs[:n_in], [split2(ref[:2 * W]) for ref in refs[n_in:n_in + n_turn]]
    outs, scratch = refs[n_in + n_turn:n_in + n_turn + len(to_hbm)], refs[n_in + n_turn + len(to_hbm):]
    held, copies = list(outs), []
    for idx, hbm in enumerate(to_hbm):
        if hbm:
            held[idx] = scratch[2 * sum(to_hbm[:idx])]
    for top, top_start, bottom, bottom_start, rows, turn, places in jobs:
        high, low = turns[turn]

        def work(begin, size, top=top, top_start=top_start, bottom=bottom, bottom_start=bottom_start):
            first = split2(blocks[top][pl.ds(top_start + begin, size)])
            second = split2(blocks[bottom][pl.ds(bottom_start + begin, size)])
            return mm3(first, (high[:W], low[:W])) + mm3(second, (high[W:], low[W:]))

        if places[0][0] >= rolled[1]:
            @pl.loop(0, rows // rolled[0])
            def _(step):
                begin = pl.multiple_of(step * rolled[0], rolled[0])
                block = work(begin, rolled[0])
                for out, start in places:
                    held[out][pl.ds(start + begin, rolled[0])] = block
        else:
            for begin in range(0, rows, BLOCK):
                block = work(begin, BLOCK)
                for out, start in places:
                    held[out][start + begin:start + begin + BLOCK] = block
        for out, start in places:
            if to_hbm[out]:
                span, sems = pl.ds(start, rows), scratch[2 * sum(to_hbm[:out]) + 1]
                copies.append(pltpu.make_async_copy(held[out].at[span], outs[out].at[span], sems.at[len(copies)]))
                copies[-1].start()
    for source, start, rows, out, out_start in moves:
        held[out][out_start:out_start + rows] = refs[source][start:start + rows]
    for copy in copies:
        copy.wait()


def rotated(jobs, outs, moves=(), after=(), rolled=(BLOCK, 9)):
    arrays, turns = [], []

    def index(array, known):
        for idx, other in enumerate(known):
            if other is array:
                return idx
        known.append(array)
        return len(known) - 1

    listed, count = [], 0
    for top, top_start, bottom, bottom_start, rows, turn, places in jobs:
        count += rows
        listed.append((index(top, arrays), top_start, index(bottom, arrays), bottom_start, rows, index(turn, turns),
                       tuple(places)))
    copied = [(index(array, arrays), start, rows, out, row) for array, start, rows, out, row in moves]
    scratch = []
    for rows, hbm in outs:
        if hbm:
            scratch += [pltpu.VMEM((rows, W), F32), pltpu.SemaphoreType.DMA((8,))]
    result = pl.pallas_call(
        functools.partial(apply_kernel, listed, copied, len(arrays), len(turns), len(after), [hbm for _, hbm in outs], rolled),
        out_shape=[jax.ShapeDtypeStruct((rows, W), F32) for rows, _ in outs],
        in_specs=[IN_VMEM] * (len(arrays) + len(turns)) + [ANYWHERE] * len(after),
        out_specs=[IN_HBM if hbm else IN_VMEM for _, hbm in outs],
        scratch_shapes=scratch,
        compiler_params=granted(12),
        cost_estimate=pl.CostEstimate(flops=6 * 2 * W * W * count, bytes_accessed=12 * W * count, transcendentals=0),
    )(*arrays, *turns, *after)
    return result


def sum_kernel(count, *refs):
    refs[-1][...] = functools.reduce(lambda a, b: a + b, [ref[...] for ref in refs[:count]])


def summed(terms, after):
    return pl.pallas_call(
        functools.partial(sum_kernel, len(terms)),
        out_shape=jax.ShapeDtypeStruct(terms[0].shape, F32),
        in_specs=[IN_VMEM] * len(terms) + [ANYWHERE] * len(after),
        out_specs=IN_VMEM,
        compiler_params=granted(2),
    )(*terms, *after)


def tie_kernel(*refs):
    pass


def tied(array, after):
    return pl.pallas_call(
        tie_kernel,
        out_shape=jax.ShapeDtypeStruct(array.shape, F32),
        in_specs=[ANYWHERE] * (1 + len(after)),
        out_specs=ANYWHERE,
        input_output_aliases={0: 0},
        compiler_params=granted(1),
    )(array, *after)


def last_kernel(count, *refs):
    parts, out_ref, sems = refs[:count], refs[count + 1], refs[count + 2]
    at, copies = out_ref.shape[0], []
    for idx in reversed(range(count)):
        rows = parts[idx].shape[0]
        at -= rows
        copies.append(pltpu.make_async_copy(parts[idx], out_ref.at[pl.ds(at, rows)], sems.at[idx]))
        copies[-1].start()
    for copy in copies:
        copy.wait()


def with_last(whole, parts):
    return pl.pallas_call(
        functools.partial(last_kernel, len(parts)),
        out_shape=jax.ShapeDtypeStruct(whole.shape, F32),
        in_specs=[IN_VMEM] * len(parts) + [IN_HBM],
        out_specs=IN_HBM,
        scratch_shapes=[pltpu.SemaphoreType.DMA((len(parts),))],
        input_output_aliases={len(parts): 0},
        compiler_params=granted(2),
    )(*parts, whole)


def passed_along(array, by=1):
    length = lax.axis_size("pair")
    return lax.ppermute(array, "pair", [(i, (i + by) % length) for i in range(length)])


def along_y(array, by):
    length = lax.axis_size("row") // 2
    return lax.ppermute(
        array, "row", [(2 * y + h, 2 * ((y + by) % length) + h) for y in range(length) for h in range(2)]
    )


def across_x(array):
    return lax.ppermute(array, "row", [(i, i ^ 1) for i in range(lax.axis_size("row"))])


def scattered(pieces, after):
    return summed([pieces[0]] + [along_y(pieces[r], r) for r in (1, 2, 3)], after)


def gathered_quarters(total):
    return [total] + [along_y(total, r) for r in (1, 2, 3)]


def on_device(top, bottom):
    where = (lax.axis_index("row") // 2).astype(jnp.int32).reshape(1)
    rows = top.shape[0]
    late = rows - RAW
    mid = late - LAST

    own_a = loaded(top, bottom, RAW)
    raw = passed_along(own_a)
    *pieces, own_b = first_gram(where, own_a, top, bottom)
    total = scattered(pieces, [])
    total = summed([total, across_x(total)], [raw])
    total_prev = passed_along(total)
    first, second, whole = rotation(where, gathered_quarters(total))
    (sent,) = rotated([(own_b, 0, own_b, late, late, first, [(0, 0)])], [(late, False)], after=[total_prev], rolled=(BLOCK, 0))
    quarters_prev = gathered_quarters(tied(total_prev, [sent]))
    sent = passed_along(sent)
    (bottom,) = rotated(
        [(own_a, 0, own_a, RAW, RAW, second, [(0, 0)]), (own_b, 0, own_b, late, late, second, [(0, RAW)])],
        [(rows, False)],
        rolled=(BLOCK, 0),
    )
    (bottom_gram,) = turned_grams(whole, second)
    first_prev, second_prev, whole_prev = rotation(where, quarters_prev, [bottom_gram])
    (early,) = rotated(
        [(raw, 0, raw, RAW, RAW, first_prev, [(0, 0)])], [(RAW + MORE, False)], [(bottom, RAW, MORE, 0, RAW)],
        rolled=(BLOCK, 0),
    )
    early_prev = passed_along(early)
    (top_gram,) = turned_grams(whole_prev, first_prev)

    *pieces, ship = late_cross(
        where, sent, bottom, early_cross(early, bottom), mid, []
    )
    total = scattered(pieces, [early_prev, top_gram])
    total = total + across_x(total)
    ship = passed_along(tied(ship, [total]))
    (bottom_prev,) = rotated(
        [(raw, 0, raw, RAW, RAW, second_prev, [(0, 0)])], [(RAW, False)], rolled=(BLOCK, 0)
    )
    first, second = second_rotation(where, gathered_quarters(total), top_gram, bottom_gram)
    first_prev = passed_along(first)
    *out_late, bottom_out = rotated(
        [
            (sent, mid, bottom, RAW + mid, LAST - W, first, [(0, 0)]),
            (sent, late - W, bottom, rows - W, W, first, [(1, 0)]),
            (early, 0, bottom, 0, RAW, second, [(2, 0)]),
            (sent, 0, bottom, RAW, late, second, [(2, RAW)]),
        ],
        [(LAST - W, False), (W, False), (rows, True)],
        rolled=(BLOCK, 2),
    )
    out_late = [passed_along(part) for part in out_late]
    (top_out,) = rotated(
        [
            (early_prev, 0, bottom_prev, 0, RAW, first_prev, [(0, 0)]),
            (ship, 0, early_prev, RAW, MORE, first_prev, [(0, RAW)]),
            (ship, MORE, ship, mid, mid - MORE, first_prev, [(0, RAW + MORE)]),
        ],
        [(rows, True)],
        rolled=(BLOCK, 0),
    )
    return (with_last(top_out, out_late), bottom_out)


def solution(mesh):
    placed = (P("row", "pair"), P("row", "pair"))
    return jax.shard_map(on_device, mesh=mesh, in_specs=placed, out_specs=placed, check_vma=False)
```

```python
import functools

import jax
import jax.numpy as jnp
from jax import lax
from jax.experimental import pallas as pl
from jax.experimental.pallas import tpu as pltpu
from jax.sharding import PartitionSpec as P

STEPS = 2
SWEEPS = 3
W = 256
H = 128
PIECE = 2 * H + 8
Q = W // 4
CROSS = Q + 8
RAW = 512
MORE = 256
LAST = 768
BLOCK = 256
BF, F32 = jnp.bfloat16, jnp.float32
IN_VMEM = pl.BlockSpec(memory_space=pltpu.VMEM)
IN_SMEM = pl.BlockSpec(memory_space=pltpu.SMEM)
IN_HBM = pl.BlockSpec(memory_space=pltpu.HBM)
ANYWHERE = pl.BlockSpec(memory_space=pl.ANY)
MIB = 1024 * 1024


def granted(mib):
    return pltpu.CompilerParams(vmem_limit_bytes=mib * MIB)


def split2(x):
    high = x.astype(BF)
    return high, (x - high.astype(F32)).astype(BF)


def dot_tn(left, right):
    return lax.dot_general(left, right, (((0,), (0,)), ((), ())), preferred_element_type=F32)


def dot_nn(left, right):
    return jnp.dot(left, right, preferred_element_type=F32)


def mm3(left, right, dot=dot_nn):
    lh, ll = left
    rh, rl = right
    return dot(lh, rh) + (dot(lh, rl) + dot(ll, rh))


def mm1(left, right):
    return dot_nn(left[0], right[0])


def iotas(shape):
    return lax.broadcasted_iota(jnp.int32, shape, 0), lax.broadcasted_iota(jnp.int32, shape, 1)


def add_rows(accs, top, bottom, begin):
    th, tl = split2(top)
    bh, bl = split2(bottom)
    shares = (
        dot_tn(th, th),
        dot_tn(th, tl),
        dot_tn(bh, bh),
        dot_tn(bh, bl),
        dot_tn(th, bh) + (dot_tn(th, bl) + dot_tn(tl, bh)),
    )
    for acc, share in zip(accs, shares):
        acc[...] = share if begin else acc[...] + share


def put_pieces(accs, pieces, outs, mine):
    xtt, ytt, xbb, ybb, tb = accs
    row, col = iotas((H, H))
    upper, diag = row <= col, row == col
    for idx, (x, y) in enumerate(((xtt, ytt), (xbb, ybb))):
        full = x[...] + (y[...] + y[...].T)
        first, last = full[:H, :H], full[H:, H:]
        pieces[idx, 0:H] = full[:H, H:]
        pieces[idx, H:2 * H] = jnp.where(upper, first, last)
        line = jnp.sum(jnp.where(diag, last, 0.0), axis=0, keepdims=True)
        pieces[idx, 2 * H:PIECE] = jnp.broadcast_to(line, (8, H))
    for idx in range(2):
        half = tb[idx * H:(idx + 1) * H, :]
        pieces[2 + idx, 0:H] = half[:, :H]
        pieces[2 + idx, H:2 * H] = half[:, H:]
        pieces[2 + idx, 2 * H:PIECE] = jnp.zeros((8, H), F32)
    for ahead in range(4):
        outs[ahead][...] = pieces[(mine + ahead) % 4]


ACCS = [pltpu.VMEM((W, W), F32)] * 5
PIECES = pltpu.VMEM((4, PIECE, H), F32)


def load_kernel(top_ref, bottom_ref, out_ref, sems):
    rows = out_ref.shape[0] // 2
    copies = [
        pltpu.make_async_copy(ref.at[pl.ds(0, rows)], out_ref.at[pl.ds(side * rows, rows)], sems.at[side])
        for side, ref in enumerate((top_ref, bottom_ref))
    ]
    for copy in copies:
        copy.start()
    for copy in copies:
        copy.wait()


def loaded(top, bottom, rows):
    return pl.pallas_call(
        load_kernel,
        out_shape=jax.ShapeDtypeStruct((2 * rows, W), F32),
        in_specs=[IN_HBM, IN_HBM],
        out_specs=IN_VMEM,
        scratch_shapes=[pltpu.SemaphoreType.DMA((2,))],
        compiler_params=granted(51),
        cost_estimate=pl.CostEstimate(flops=0, bytes_accessed=16 * W * rows, transcendentals=0),
    )(top, bottom)


def first_gram_kernel(where_ref, loaded_ref, top_ref, bottom_ref, *refs):
    outs, rest, accs, pieces, sems = refs[:4], refs[4], refs[5:10], refs[10], refs[11]
    size, rows = loaded_ref.shape[0] // 2, rest.shape[0] // 2

    def copies(part):
        start = pl.multiple_of(part * size, size)
        return [
            pltpu.make_async_copy(
                ref.at[pl.ds(pl.multiple_of(start + size, size), size)],
                rest.at[pl.ds(pl.multiple_of(side * rows + start, size), size)],
                sems.at[2 * part + side],
            )
            for side, ref in enumerate((top_ref, bottom_ref))
        ]

    for part in range(rows // size):
        for copy in copies(part):
            copy.start()
    for acc in accs:
        acc[...] = jnp.zeros_like(acc)

    @pl.loop(0, size // BLOCK)
    def _(step):
        start = pl.multiple_of(step * BLOCK, BLOCK)
        add_rows(accs, loaded_ref[pl.ds(start, BLOCK)], loaded_ref[pl.ds(size + start, BLOCK)], False)

    @pl.loop(0, rows // size)
    def _(part):
        for copy in copies(part):
            copy.wait()

        @pl.loop(0, size // BLOCK)
        def _(step):
            start = pl.multiple_of(part * size + step * BLOCK, BLOCK)
            add_rows(accs, rest[pl.ds(start, BLOCK)], rest[pl.ds(rows + start, BLOCK)], False)

    put_pieces(accs, pieces, outs, where_ref[0])


def first_gram(where, own_a, top, bottom):
    rest = 2 * top.shape[0] - own_a.shape[0]
    return pl.pallas_call(
        first_gram_kernel,
        out_shape=[jax.ShapeDtypeStruct((PIECE, H), F32)] * 4 + [jax.ShapeDtypeStruct((rest, W), F32)],
        in_specs=[IN_SMEM, IN_VMEM, IN_HBM, IN_HBM],
        out_specs=[IN_VMEM] * 5,
        scratch_shapes=ACCS + [PIECES, pltpu.SemaphoreType.DMA((2 * rest // own_a.shape[0],))],
        compiler_params=granted(51),
        cost_estimate=pl.CostEstimate(flops=7 * 2 * W * W * 2048, bytes_accessed=2 ** 22, transcendentals=0),
    )(where, own_a, top, bottom)


def add_cross(cross, squares, top, bottom, begin):
    th, tl = split2(top)
    bh, bl = split2(bottom)
    share = dot_tn(th, bh) + (dot_tn(th, bl) + dot_tn(tl, bh))
    cross[...] = share if begin else cross[...] + share
    for idx, block in enumerate((top, bottom)):
        share = jnp.sum(block * block, axis=0, keepdims=True)
        squares[idx:idx + 1] = share if begin else squares[idx:idx + 1] + share


def early_cross_kernel(top_ref, bottom_ref, cross, squares):
    squares[...] = jnp.zeros_like(squares)
    add_cross(cross, squares, top_ref[:RAW], bottom_ref[:RAW], True)


def early_cross(top, bottom):
    return pl.pallas_call(
        early_cross_kernel,
        out_shape=[jax.ShapeDtypeStruct((W, W), F32), jax.ShapeDtypeStruct((8, W), F32)],
        in_specs=[IN_VMEM, IN_VMEM],
        out_specs=[IN_VMEM] * 2,
        compiler_params=granted(12),
        cost_estimate=pl.CostEstimate(flops=3 * 2 * W * W * 1024, bytes_accessed=2 ** 21, transcendentals=0),
    )(top, bottom)


def late_cross_kernel(count, where_ref, top_ref, bottom_ref, cross_ref, squares_ref, *refs):
    refs = refs[count:]
    outs, ship, cross, squares, pieces, sems = refs[:4], refs[4], refs[5], refs[6], refs[7], refs[8]
    late = top_ref.shape[0]
    early, mid = bottom_ref.shape[0] - late, (ship.shape[0] + MORE) // 2
    copies = [
        pltpu.make_async_copy(top_ref.at[pl.ds(0, mid)], ship.at[pl.ds(0, mid)], sems.at[0]),
        pltpu.make_async_copy(
            bottom_ref.at[pl.ds(early + MORE, mid - MORE)], ship.at[pl.ds(mid, mid - MORE)], sems.at[1]
        ),
    ]
    for copy in copies:
        copy.start()
    cross[...] = cross_ref[...]
    squares[...] = squares_ref[...]

    @pl.loop(0, top_ref.shape[0] // BLOCK)
    def _(step):
        begin = pl.multiple_of(step * BLOCK, BLOCK)
        add_cross(cross, squares, top_ref[pl.ds(begin, BLOCK)], bottom_ref[pl.ds(early + begin, BLOCK)], False)

    for idx in range(4):
        pieces[idx, :Q] = cross[idx * Q:(idx + 1) * Q]
        pieces[idx, Q:] = squares[...] if idx == 0 else jnp.zeros_like(squares)
    for ahead in range(4):
        outs[ahead][...] = pieces[(where_ref[0] + ahead) % 4]
    for copy in copies:
        copy.wait()


def late_cross(where, top, bottom, before, mid, after):
    return pl.pallas_call(
        functools.partial(late_cross_kernel, len(after)),
        out_shape=[jax.ShapeDtypeStruct((CROSS, W), F32)] * 4 + [jax.ShapeDtypeStruct((2 * mid - MORE, W), F32)],
        in_specs=[IN_SMEM] + [IN_VMEM] * 4 + [ANYWHERE] * len(after),
        out_specs=[IN_VMEM] * 5,
        scratch_shapes=[
            pltpu.VMEM((W, W), F32), pltpu.VMEM((8, W), F32), pltpu.VMEM((4, CROSS, W), F32),
            pltpu.SemaphoreType.DMA((2,)),
        ],
        compiler_params=granted(12),
        cost_estimate=pl.CostEstimate(flops=3 * 2 * W * W * 1024, bytes_accessed=2 ** 21, transcendentals=0),
    )(where, top, bottom, *before, *after)


def turned_gram_kernel(count, gram_ref, *refs):
    whole = split2(gram_ref[...])
    for ref, out in zip(refs[:count], refs[count:]):
        turn = split2(ref[...])
        out[...] = mm3(turn, split2(mm3(whole, turn)), dot_tn)


def turned_grams(gram, *turns):
    return pl.pallas_call(
        functools.partial(turned_gram_kernel, len(turns)),
        out_shape=[jax.ShapeDtypeStruct((W, W), F32)] * len(turns),
        in_specs=[IN_VMEM] * (1 + len(turns)),
        out_specs=[IN_VMEM] * len(turns),
        compiler_params=granted(16),
        cost_estimate=pl.CostEstimate(flops=3 * (2 * W) ** 3 * len(turns), bytes_accessed=2 ** 21, transcendentals=0),
    )(gram, *turns)


def turn_columns(gram, sq_line, sq_col):
    sq_line, sq_col = sq_line + 1e-06, sq_col + 1e-06
    corr = gram * (1.0 / jnp.sqrt(sq_col)) * (1.0 / jnp.sqrt(sq_line))
    generator = corr * ((sq_line - sq_col) / (sq_line + sq_col))
    frobenius = jnp.sqrt(jnp.sum(generator * generator))
    skew = generator * (1.0 / (1.0 + frobenius))

    s2 = split2(skew)
    n = -mm3(s2, s2)
    n_2 = split2(n)
    nn = mm3(n_2, n_2)
    d1 = 0.25 * mm1(split2(nn), n_2) - 0.75 * nn
    d1_2 = split2(d1)
    dd = mm1(d1_2, d1_2)
    d2 = 0.25 * mm1(split2(dd), d1_2) - 0.75 * dd
    x = 0.5 * (d1 + d2) - 0.25 * mm1(d1_2, split2(d2))
    y = 0.5 * n + x - 0.5 * mm1(n_2, split2(x))
    row, col = iotas((2 * W, 2 * W))
    return jnp.where(row == col, 1.0, skew) - (y + mm3(s2, split2(y)))


def rotation_kernel(where_ref, q0, q1, q2, q3, *refs):
    first_ref, second_ref, gram, pieces = refs[-4:]
    mine = where_ref[0]
    for behind, piece in enumerate((q0, q1, q2, q3)):
        pieces[(mine + 4 - behind) % 4] = piece[...]
    row, col = iotas((H, H))
    upper, diag = row <= col, row == col

    def put(i, j, block):
        gram[i * H:(i + 1) * H, j * H:(j + 1) * H] = block

    lines, columns = [], []
    for half in range(2):
        off = pieces[half, 0:H]
        both = pieces[half, H:2 * H]
        line = pieces[half, 2 * H:2 * H + 1]
        turned = both.T
        first = jnp.where(upper, both, turned)
        last = jnp.where(diag, line, jnp.where(upper, turned, both))
        a, b = 2 * half, 2 * half + 1
        put(a, b, off)
        put(b, a, off.T)
        put(a, a, first)
        put(b, b, last)
        for block in (first, last):
            on = jnp.where(diag, block, 0.0)
            lines.append(jnp.sum(on, axis=0, keepdims=True))
            columns.append(jnp.sum(on, axis=1, keepdims=True))
    for i in range(2):
        for j in range(2):
            block = pieces[2 + i, j * H:(j + 1) * H]
            put(i, 2 + j, block)
            put(2 + j, i, block.T)
    rotate = turn_columns(gram[...], jnp.concatenate(lines, axis=1), jnp.concatenate(columns, axis=0))
    first_ref[...] = rotate[:, :W]
    second_ref[...] = rotate[:, W:]


def rotation(where, quarters, after=()):
    half = jax.ShapeDtypeStruct((2 * W, W), F32)
    return pl.pallas_call(
        rotation_kernel,
        out_shape=[half, half, jax.ShapeDtypeStruct((2 * W, 2 * W), F32)],
        in_specs=[IN_SMEM] + [IN_VMEM] * 4 + [ANYWHERE] * len(after),
        out_specs=[IN_VMEM] * 3,
        scratch_shapes=[PIECES],
        compiler_params=granted(20),
        cost_estimate=pl.CostEstimate(flops=14 * 2 * (2 * W) ** 3, bytes_accessed=2 ** 21, transcendentals=0),
    )(where, *quarters, *after)


def second_rotation_kernel(where_ref, q0, q1, q2, q3, top_ref, bottom_ref, first_ref, second_ref, pieces, gram):
    mine = where_ref[0]
    for behind, piece in enumerate((q0, q1, q2, q3)):
        pieces[(mine + 4 - behind) % 4] = piece[...]
    for idx in range(4):
        rows = slice(idx * Q, (idx + 1) * Q)
        gram[rows, W:] = pieces[idx, :Q]
    gram[:W, :W] = top_ref[...]
    gram[W:, W:] = bottom_ref[...]
    gram[W:, :W] = gram[:W, W:].T
    row, col = iotas((W, W))
    lines, columns = [], []
    for idx in range(2):
        line = pieces[0, Q + idx:Q + idx + 1]
        lines.append(line)
        columns.append(jnp.sum(jnp.where(row == col, line, 0.0), axis=1, keepdims=True))
    rotate = turn_columns(gram[...], jnp.concatenate(lines, axis=1), jnp.concatenate(columns, axis=0))
    first_ref[...] = rotate[:, :W]
    second_ref[...] = rotate[:, W:]


def second_rotation(where, quarters, top_gram, bottom_gram):
    half = jax.ShapeDtypeStruct((2 * W, W), F32)
    return pl.pallas_call(
        second_rotation_kernel,
        out_shape=[half, half],
        in_specs=[IN_SMEM] + [IN_VMEM] * 6,
        out_specs=[IN_VMEM] * 2,
        scratch_shapes=[pltpu.VMEM((4, CROSS, W), F32), pltpu.VMEM((2 * W, 2 * W), F32)],
        compiler_params=granted(20),
        cost_estimate=pl.CostEstimate(flops=14 * 2 * (2 * W) ** 3, bytes_accessed=2 ** 21, transcendentals=0),
    )(where, *quarters, top_gram, bottom_gram)


def apply_kernel(jobs, moves, n_in, n_turn, n_after, to_hbm, rolled, *refs):
    refs = refs[:n_in + n_turn] + refs[n_in + n_turn + n_after:]
    blocks, turns = refs[:n_in], [split2(ref[:2 * W]) for ref in refs[n_in:n_in + n_turn]]
    outs, scratch = refs[n_in + n_turn:n_in + n_turn + len(to_hbm)], refs[n_in + n_turn + len(to_hbm):]
    held, copies = list(outs), []
    for idx, hbm in enumerate(to_hbm):
        if hbm:
            held[idx] = scratch[2 * sum(to_hbm[:idx])]
    for top, top_start, bottom, bottom_start, rows, turn, places in jobs:
        high, low = turns[turn]

        def work(begin, size, top=top, top_start=top_start, bottom=bottom, bottom_start=bottom_start):
            first = split2(blocks[top][pl.ds(top_start + begin, size)])
            second = split2(blocks[bottom][pl.ds(bottom_start + begin, size)])
            return mm3(first, (high[:W], low[:W])) + mm3(second, (high[W:], low[W:]))

        if places[0][0] >= rolled[1]:
            @pl.loop(0, rows // rolled[0])
            def _(step):
                begin = pl.multiple_of(step * rolled[0], rolled[0])
                block = work(begin, rolled[0])
                for out, start in places:
                    held[out][pl.ds(start + begin, rolled[0])] = block
        else:
            for begin in range(0, rows, BLOCK):
                block = work(begin, BLOCK)
                for out, start in places:
                    held[out][start + begin:start + begin + BLOCK] = block
        for out, start in places:
            if to_hbm[out]:
                span, sems = pl.ds(start, rows), scratch[2 * sum(to_hbm[:out]) + 1]
                copies.append(pltpu.make_async_copy(held[out].at[span], outs[out].at[span], sems.at[len(copies)]))
                copies[-1].start()
    for source, start, rows, out, out_start in moves:
        held[out][out_start:out_start + rows] = refs[source][start:start + rows]
    for copy in copies:
        copy.wait()


def rotated(jobs, outs, moves=(), after=(), rolled=(BLOCK, 9)):
    arrays, turns = [], []

    def index(array, known):
        for idx, other in enumerate(known):
            if other is array:
                return idx
        known.append(array)
        return len(known) - 1

    listed, count = [], 0
    for top, top_start, bottom, bottom_start, rows, turn, places in jobs:
        count += rows
        listed.append((index(top, arrays), top_start, index(bottom, arrays), bottom_start, rows, index(turn, turns),
                       tuple(places)))
    copied = [(index(array, arrays), start, rows, out, row) for array, start, rows, out, row in moves]
    scratch = []
    for rows, hbm in outs:
        if hbm:
            scratch += [pltpu.VMEM((rows, W), F32), pltpu.SemaphoreType.DMA((8,))]
    result = pl.pallas_call(
        functools.partial(apply_kernel, listed, copied, len(arrays), len(turns), len(after), [hbm for _, hbm in outs], rolled),
        out_shape=[jax.ShapeDtypeStruct((rows, W), F32) for rows, _ in outs],
        in_specs=[IN_VMEM] * (len(arrays) + len(turns)) + [ANYWHERE] * len(after),
        out_specs=[IN_HBM if hbm else IN_VMEM for _, hbm in outs],
        scratch_shapes=scratch,
        compiler_params=granted(12),
        cost_estimate=pl.CostEstimate(flops=6 * 2 * W * W * count, bytes_accessed=12 * W * count, transcendentals=0),
    )(*arrays, *turns, *after)
    return result


def sum_kernel(count, *refs):
    refs[-1][...] = functools.reduce(lambda a, b: a + b, [ref[...] for ref in refs[:count]])


def summed(terms, after):
    return pl.pallas_call(
        functools.partial(sum_kernel, len(terms)),
        out_shape=jax.ShapeDtypeStruct(terms[0].shape, F32),
        in_specs=[IN_VMEM] * len(terms) + [ANYWHERE] * len(after),
        out_specs=IN_VMEM,
        compiler_params=granted(2),
    )(*terms, *after)


def tie_kernel(*refs):
    pass


def tied(array, after):
    return pl.pallas_call(
        tie_kernel,
        out_shape=jax.ShapeDtypeStruct(array.shape, F32),
        in_specs=[ANYWHERE] * (1 + len(after)),
        out_specs=ANYWHERE,
        input_output_aliases={0: 0},
        compiler_params=granted(1),
    )(array, *after)


def last_kernel(count, *refs):
    parts, out_ref, sems = refs[:count], refs[count + 1], refs[count + 2]
    at, copies = out_ref.shape[0], []
    for idx in reversed(range(count)):
        rows = parts[idx].shape[0]
        at -= rows
        copies.append(pltpu.make_async_copy(parts[idx], out_ref.at[pl.ds(at, rows)], sems.at[idx]))
        copies[-1].start()
    for copy in copies:
        copy.wait()


def with_last(whole, parts):
    return pl.pallas_call(
        functools.partial(last_kernel, len(parts)),
        out_shape=jax.ShapeDtypeStruct(whole.shape, F32),
        in_specs=[IN_VMEM] * len(parts) + [IN_HBM],
        out_specs=IN_HBM,
        scratch_shapes=[pltpu.SemaphoreType.DMA((len(parts),))],
        input_output_aliases={len(parts): 0},
        compiler_params=granted(2),
    )(*parts, whole)


def passed_along(array, by=1):
    length = lax.axis_size("pair")
    return lax.ppermute(array, "pair", [(i, (i + by) % length) for i in range(length)])


def along_y(array, by):
    length = lax.axis_size("row") // 2
    return lax.ppermute(
        array, "row", [(2 * y + h, 2 * ((y + by) % length) + h) for y in range(length) for h in range(2)]
    )


def across_x(array):
    return lax.ppermute(array, "row", [(i, i ^ 1) for i in range(lax.axis_size("row"))])


def scattered(pieces, after):
    return summed([pieces[0]] + [along_y(pieces[r], r) for r in (1, 2, 3)], after)


def gathered_quarters(total):
    return [total] + [along_y(total, r) for r in (1, 2, 3)]


def on_device(top, bottom):
    where = (lax.axis_index("row") // 2).astype(jnp.int32).reshape(1)
    rows = top.shape[0]
    late = rows - RAW
    mid = late - LAST

    own_a = loaded(top, bottom, RAW)
    raw = passed_along(own_a)
    *pieces, own_b = first_gram(where, own_a, top, bottom)
    total = scattered(pieces, [])
    total = summed([total, across_x(total)], [raw])
    total_prev = passed_along(total)
    first, second, whole = rotation(where, gathered_quarters(total))
    (sent,) = rotated([(own_b, 0, own_b, late, late, first, [(0, 0)])], [(late, False)], after=[total_prev], rolled=(512, 0))
    quarters_prev = gathered_quarters(tied(total_prev, [sent]))
    sent = passed_along(sent)
    (bottom,) = rotated(
        [(own_a, 0, own_a, RAW, RAW, second, [(0, 0)]), (own_b, 0, own_b, late, late, second, [(0, RAW)])],
        [(rows, False)],
        rolled=(BLOCK, 0),
    )
    (bottom_gram,) = turned_grams(whole, second)
    first_prev, second_prev, whole_prev = rotation(where, quarters_prev, [bottom_gram])
    (early,) = rotated(
        [(raw, 0, raw, RAW, RAW, first_prev, [(0, 0)])], [(RAW + MORE, False)], [(bottom, RAW, MORE, 0, RAW)],
        rolled=(BLOCK, 0),
    )
    early_prev = passed_along(early)
    (top_gram,) = turned_grams(whole_prev, first_prev)

    *pieces, ship = late_cross(
        where, sent, bottom, early_cross(early, bottom), mid, []
    )
    total = scattered(pieces, [early_prev, top_gram])
    total = total + across_x(total)
    ship = passed_along(tied(ship, [total]))
    (bottom_prev,) = rotated(
        [(raw, 0, raw, RAW, RAW, second_prev, [(0, 0)])], [(RAW, False)], rolled=(BLOCK, 0)
    )
    first, second = second_rotation(where, gathered_quarters(total), top_gram, bottom_gram)
    first_prev = passed_along(first)
    *out_late, bottom_out = rotated(
        [
            (sent, mid, bottom, RAW + mid, LAST - W, first, [(0, 0)]),
            (sent, late - W, bottom, rows - W, W, first, [(1, 0)]),
            (early, 0, bottom, 0, RAW, second, [(2, 0)]),
            (sent, 0, bottom, RAW, late, second, [(2, RAW)]),
        ],
        [(LAST - W, False), (W, False), (rows, True)],
        rolled=(BLOCK, 2),
    )
    out_late = [passed_along(part) for part in out_late]
    (top_out,) = rotated(
        [
            (early_prev, 0, bottom_prev, 0, RAW, first_prev, [(0, 0)]),
            (ship, 0, early_prev, RAW, MORE, first_prev, [(0, RAW)]),
            (ship, MORE, ship, mid, mid - MORE, first_prev, [(0, RAW + MORE)]),
        ],
        [(rows, True)],
    )
    return (with_last(top_out, out_late), bottom_out)


def solution(mesh):
    placed = (P("row", "pair"), P("row", "pair"))
    return jax.shard_map(on_device, mesh=mesh, in_specs=placed, out_specs=placed, check_vma=False)
```

```python
import functools

import jax
import jax.numpy as jnp
from jax import lax
from jax.experimental import pallas as pl
from jax.experimental.pallas import tpu as pltpu
from jax.sharding import PartitionSpec as P

STEPS = 2
SWEEPS = 3
W = 256
H = 128
PIECE = 2 * H + 8
Q = W // 4
CROSS = Q + 8
RAW = 512
MORE = 256
LAST = 768
BLOCK = 256
BF, F32 = jnp.bfloat16, jnp.float32
IN_VMEM = pl.BlockSpec(memory_space=pltpu.VMEM)
IN_SMEM = pl.BlockSpec(memory_space=pltpu.SMEM)
IN_HBM = pl.BlockSpec(memory_space=pltpu.HBM)
ANYWHERE = pl.BlockSpec(memory_space=pl.ANY)
MIB = 1024 * 1024


def granted(mib):
    return pltpu.CompilerParams(vmem_limit_bytes=mib * MIB)


def split2(x):
    high = x.astype(BF)
    return high, (x - high.astype(F32)).astype(BF)


def dot_tn(left, right):
    return lax.dot_general(left, right, (((0,), (0,)), ((), ())), preferred_element_type=F32)


def dot_nn(left, right):
    return jnp.dot(left, right, preferred_element_type=F32)


def mm3(left, right, dot=dot_nn):
    lh, ll = left
    rh, rl = right
    return dot(lh, rh) + (dot(lh, rl) + dot(ll, rh))


def mm1(left, right):
    return dot_nn(left[0], right[0])


def iotas(shape):
    return lax.broadcasted_iota(jnp.int32, shape, 0), lax.broadcasted_iota(jnp.int32, shape, 1)


def add_rows(accs, top, bottom, begin):
    th, tl = split2(top)
    bh, bl = split2(bottom)
    shares = (
        dot_tn(th, th),
        dot_tn(th, tl),
        dot_tn(bh, bh),
        dot_tn(bh, bl),
        dot_tn(th, bh) + (dot_tn(th, bl) + dot_tn(tl, bh)),
    )
    for acc, share in zip(accs, shares):
        acc[...] = share if begin else acc[...] + share


def put_pieces(accs, pieces, outs, mine):
    xtt, ytt, xbb, ybb, tb = accs
    row, col = iotas((H, H))
    upper, diag = row <= col, row == col
    for idx, (x, y) in enumerate(((xtt, ytt), (xbb, ybb))):
        full = x[...] + (y[...] + y[...].T)
        first, last = full[:H, :H], full[H:, H:]
        pieces[idx, 0:H] = full[:H, H:]
        pieces[idx, H:2 * H] = jnp.where(upper, first, last)
        line = jnp.sum(jnp.where(diag, last, 0.0), axis=0, keepdims=True)
        pieces[idx, 2 * H:PIECE] = jnp.broadcast_to(line, (8, H))
    for idx in range(2):
        half = tb[idx * H:(idx + 1) * H, :]
        pieces[2 + idx, 0:H] = half[:, :H]
        pieces[2 + idx, H:2 * H] = half[:, H:]
        pieces[2 + idx, 2 * H:PIECE] = jnp.zeros((8, H), F32)
    for ahead in range(4):
        outs[ahead][...] = pieces[(mine + ahead) % 4]


ACCS = [pltpu.VMEM((W, W), F32)] * 5
PIECES = pltpu.VMEM((4, PIECE, H), F32)


def load_kernel(top_ref, bottom_ref, out_ref, sems):
    rows = out_ref.shape[0] // 2
    copies = [
        pltpu.make_async_copy(ref.at[pl.ds(0, rows)], out_ref.at[pl.ds(side * rows, rows)], sems.at[side])
        for side, ref in enumerate((top_ref, bottom_ref))
    ]
    for copy in copies:
        copy.start()
    for copy in copies:
        copy.wait()


def loaded(top, bottom, rows):
    return pl.pallas_call(
        load_kernel,
        out_shape=jax.ShapeDtypeStruct((2 * rows, W), F32),
        in_specs=[IN_HBM, IN_HBM],
        out_specs=IN_VMEM,
        scratch_shapes=[pltpu.SemaphoreType.DMA((2,))],
        compiler_params=granted(51),
        cost_estimate=pl.CostEstimate(flops=0, bytes_accessed=16 * W * rows, transcendentals=0),
    )(top, bottom)


def first_gram_kernel(where_ref, loaded_ref, top_ref, bottom_ref, *refs):
    outs, rest, accs, pieces, sems = refs[:4], refs[4], refs[5:10], refs[10], refs[11]
    size, rows = loaded_ref.shape[0] // 2, rest.shape[0] // 2

    def copies(part):
        start = pl.multiple_of(part * size, size)
        return [
            pltpu.make_async_copy(
                ref.at[pl.ds(pl.multiple_of(start + size, size), size)],
                rest.at[pl.ds(pl.multiple_of(side * rows + start, size), size)],
                sems.at[2 * part + side],
            )
            for side, ref in enumerate((top_ref, bottom_ref))
        ]

    for part in range(rows // size):
        for copy in copies(part):
            copy.start()
    add_rows(accs, loaded_ref[:size], loaded_ref[size:], True)

    @pl.loop(0, rows // size)
    def _(part):
        for copy in copies(part):
            copy.wait()
        start = pl.multiple_of(part * size, size)
        add_rows(accs, rest[pl.ds(start, size)], rest[pl.ds(pl.multiple_of(rows + start, size), size)], False)

    put_pieces(accs, pieces, outs, where_ref[0])


def first_gram(where, own_a, top, bottom):
    rest = 2 * top.shape[0] - own_a.shape[0]
    return pl.pallas_call(
        first_gram_kernel,
        out_shape=[jax.ShapeDtypeStruct((PIECE, H), F32)] * 4 + [jax.ShapeDtypeStruct((rest, W), F32)],
        in_specs=[IN_SMEM, IN_VMEM, IN_HBM, IN_HBM],
        out_specs=[IN_VMEM] * 5,
        scratch_shapes=ACCS + [PIECES, pltpu.SemaphoreType.DMA((2 * rest // own_a.shape[0],))],
        compiler_params=granted(51),
        cost_estimate=pl.CostEstimate(flops=7 * 2 * W * W * 2048, bytes_accessed=2 ** 22, transcendentals=0),
    )(where, own_a, top, bottom)


def add_cross(cross, squares, top, bottom, begin):
    th, tl = split2(top)
    bh, bl = split2(bottom)
    share = dot_tn(th, bh) + (dot_tn(th, bl) + dot_tn(tl, bh))
    cross[...] = share if begin else cross[...] + share
    for idx, block in enumerate((top, bottom)):
        share = jnp.sum(block * block, axis=0, keepdims=True)
        squares[idx:idx + 1] = share if begin else squares[idx:idx + 1] + share


def early_cross_kernel(top_ref, bottom_ref, cross, squares):
    squares[...] = jnp.zeros_like(squares)
    add_cross(cross, squares, top_ref[:RAW], bottom_ref[:RAW], True)


def early_cross(top, bottom):
    return pl.pallas_call(
        early_cross_kernel,
        out_shape=[jax.ShapeDtypeStruct((W, W), F32), jax.ShapeDtypeStruct((8, W), F32)],
        in_specs=[IN_VMEM, IN_VMEM],
        out_specs=[IN_VMEM] * 2,
        compiler_params=granted(12),
        cost_estimate=pl.CostEstimate(flops=3 * 2 * W * W * 1024, bytes_accessed=2 ** 21, transcendentals=0),
    )(top, bottom)


def late_cross_kernel(count, where_ref, top_ref, bottom_ref, cross_ref, squares_ref, *refs):
    refs = refs[count:]
    outs, ship, cross, squares, pieces, sems = refs[:4], refs[4], refs[5], refs[6], refs[7], refs[8]
    late = top_ref.shape[0]
    early, mid = bottom_ref.shape[0] - late, (ship.shape[0] + MORE) // 2
    copies = [
        pltpu.make_async_copy(top_ref.at[pl.ds(0, mid)], ship.at[pl.ds(0, mid)], sems.at[0]),
        pltpu.make_async_copy(
            bottom_ref.at[pl.ds(early + MORE, mid - MORE)], ship.at[pl.ds(mid, mid - MORE)], sems.at[1]
        ),
    ]
    for copy in copies:
        copy.start()
    cross[...] = cross_ref[...]
    squares[...] = squares_ref[...]

    @pl.loop(0, top_ref.shape[0] // 512)
    def _(step):
        begin = pl.multiple_of(step * 512, 512)
        add_cross(cross, squares, top_ref[pl.ds(begin, 512)], bottom_ref[pl.ds(early + begin, 512)], False)

    for idx in range(4):
        pieces[idx, :Q] = cross[idx * Q:(idx + 1) * Q]
        pieces[idx, Q:] = squares[...] if idx == 0 else jnp.zeros_like(squares)
    for ahead in range(4):
        outs[ahead][...] = pieces[(where_ref[0] + ahead) % 4]
    for copy in copies:
        copy.wait()


def late_cross(where, top, bottom, before, mid, after):
    return pl.pallas_call(
        functools.partial(late_cross_kernel, len(after)),
        out_shape=[jax.ShapeDtypeStruct((CROSS, W), F32)] * 4 + [jax.ShapeDtypeStruct((2 * mid - MORE, W), F32)],
        in_specs=[IN_SMEM] + [IN_VMEM] * 4 + [ANYWHERE] * len(after),
        out_specs=[IN_VMEM] * 5,
        scratch_shapes=[
            pltpu.VMEM((W, W), F32), pltpu.VMEM((8, W), F32), pltpu.VMEM((4, CROSS, W), F32),
            pltpu.SemaphoreType.DMA((2,)),
        ],
        compiler_params=granted(12),
        cost_estimate=pl.CostEstimate(flops=3 * 2 * W * W * 1024, bytes_accessed=2 ** 21, transcendentals=0),
    )(where, top, bottom, *before, *after)


def turned_gram_kernel(count, gram_ref, *refs):
    whole = split2(gram_ref[...])
    for ref, out in zip(refs[:count], refs[count:]):
        turn = split2(ref[...])
        out[...] = mm3(turn, split2(mm3(whole, turn)), dot_tn)


def turned_grams(gram, *turns):
    return pl.pallas_call(
        functools.partial(turned_gram_kernel, len(turns)),
        out_shape=[jax.ShapeDtypeStruct((W, W), F32)] * len(turns),
        in_specs=[IN_VMEM] * (1 + len(turns)),
        out_specs=[IN_VMEM] * len(turns),
        compiler_params=granted(16),
        cost_estimate=pl.CostEstimate(flops=3 * (2 * W) ** 3 * len(turns), bytes_accessed=2 ** 21, transcendentals=0),
    )(gram, *turns)


def turn_columns(gram, sq_line, sq_col):
    sq_line, sq_col = sq_line + 1e-06, sq_col + 1e-06
    corr = gram * (1.0 / jnp.sqrt(sq_col)) * (1.0 / jnp.sqrt(sq_line))
    generator = corr * ((sq_line - sq_col) / (sq_line + sq_col))
    frobenius = jnp.sqrt(jnp.sum(generator * generator))
    skew = generator * (1.0 / (1.0 + frobenius))

    s2 = split2(skew)
    n = -mm3(s2, s2)
    n_2 = split2(n)
    nn = mm3(n_2, n_2)
    d1 = 0.25 * mm1(split2(nn), n_2) - 0.75 * nn
    d1_2 = split2(d1)
    dd = mm1(d1_2, d1_2)
    d2 = 0.25 * mm1(split2(dd), d1_2) - 0.75 * dd
    x = 0.5 * (d1 + d2) - 0.25 * mm1(d1_2, split2(d2))
    y = 0.5 * n + x - 0.5 * mm1(n_2, split2(x))
    row, col = iotas((2 * W, 2 * W))
    return jnp.where(row == col, 1.0, skew) - (y + mm3(s2, split2(y)))


def rotation_kernel(where_ref, q0, q1, q2, q3, *refs):
    first_ref, second_ref, gram, pieces = refs[-4:]
    mine = where_ref[0]
    for behind, piece in enumerate((q0, q1, q2, q3)):
        pieces[(mine + 4 - behind) % 4] = piece[...]
    row, col = iotas((H, H))
    upper, diag = row <= col, row == col

    def put(i, j, block):
        gram[i * H:(i + 1) * H, j * H:(j + 1) * H] = block

    lines, columns = [], []
    for half in range(2):
        off = pieces[half, 0:H]
        both = pieces[half, H:2 * H]
        line = pieces[half, 2 * H:2 * H + 1]
        turned = both.T
        first = jnp.where(upper, both, turned)
        last = jnp.where(diag, line, jnp.where(upper, turned, both))
        a, b = 2 * half, 2 * half + 1
        put(a, b, off)
        put(b, a, off.T)
        put(a, a, first)
        put(b, b, last)
        for block in (first, last):
            on = jnp.where(diag, block, 0.0)
            lines.append(jnp.sum(on, axis=0, keepdims=True))
            columns.append(jnp.sum(on, axis=1, keepdims=True))
    for i in range(2):
        for j in range(2):
            block = pieces[2 + i, j * H:(j + 1) * H]
            put(i, 2 + j, block)
            put(2 + j, i, block.T)
    rotate = turn_columns(gram[...], jnp.concatenate(lines, axis=1), jnp.concatenate(columns, axis=0))
    first_ref[...] = rotate[:, :W]
    second_ref[...] = rotate[:, W:]


def rotation(where, quarters, after=()):
    half = jax.ShapeDtypeStruct((2 * W, W), F32)
    return pl.pallas_call(
        rotation_kernel,
        out_shape=[half, half, jax.ShapeDtypeStruct((2 * W, 2 * W), F32)],
        in_specs=[IN_SMEM] + [IN_VMEM] * 4 + [ANYWHERE] * len(after),
        out_specs=[IN_VMEM] * 3,
        scratch_shapes=[PIECES],
        compiler_params=granted(20),
        cost_estimate=pl.CostEstimate(flops=14 * 2 * (2 * W) ** 3, bytes_accessed=2 ** 21, transcendentals=0),
    )(where, *quarters, *after)


def second_rotation_kernel(where_ref, q0, q1, q2, q3, top_ref, bottom_ref, first_ref, second_ref, pieces, gram):
    mine = where_ref[0]
    for behind, piece in enumerate((q0, q1, q2, q3)):
        pieces[(mine + 4 - behind) % 4] = piece[...]
    for idx in range(4):
        rows = slice(idx * Q, (idx + 1) * Q)
        gram[rows, W:] = pieces[idx, :Q]
    gram[:W, :W] = top_ref[...]
    gram[W:, W:] = bottom_ref[...]
    gram[W:, :W] = gram[:W, W:].T
    row, col = iotas((W, W))
    lines, columns = [], []
    for idx in range(2):
        line = pieces[0, Q + idx:Q + idx + 1]
        lines.append(line)
        columns.append(jnp.sum(jnp.where(row == col, line, 0.0), axis=1, keepdims=True))
    rotate = turn_columns(gram[...], jnp.concatenate(lines, axis=1), jnp.concatenate(columns, axis=0))
    first_ref[...] = rotate[:, :W]
    second_ref[...] = rotate[:, W:]


def second_rotation(where, quarters, top_gram, bottom_gram):
    half = jax.ShapeDtypeStruct((2 * W, W), F32)
    return pl.pallas_call(
        second_rotation_kernel,
        out_shape=[half, half],
        in_specs=[IN_SMEM] + [IN_VMEM] * 6,
        out_specs=[IN_VMEM] * 2,
        scratch_shapes=[pltpu.VMEM((4, CROSS, W), F32), pltpu.VMEM((2 * W, 2 * W), F32)],
        compiler_params=granted(20),
        cost_estimate=pl.CostEstimate(flops=14 * 2 * (2 * W) ** 3, bytes_accessed=2 ** 21, transcendentals=0),
    )(where, *quarters, top_gram, bottom_gram)


def apply_kernel(jobs, moves, n_in, n_turn, n_after, to_hbm, rolled, *refs):
    refs = refs[:n_in + n_turn] + refs[n_in + n_turn + n_after:]
    blocks, turns = refs[:n_in], [split2(ref[:2 * W]) for ref in refs[n_in:n_in + n_turn]]
    outs, scratch = refs[n_in + n_turn:n_in + n_turn + len(to_hbm)], refs[n_in + n_turn + len(to_hbm):]
    held, copies = list(outs), []
    for idx, hbm in enumerate(to_hbm):
        if hbm:
            held[idx] = scratch[2 * sum(to_hbm[:idx])]
    for top, top_start, bottom, bottom_start, rows, turn, places in jobs:
        high, low = turns[turn]

        def work(begin, size, top=top, top_start=top_start, bottom=bottom, bottom_start=bottom_start):
            first = split2(blocks[top][pl.ds(top_start + begin, size)])
            second = split2(blocks[bottom][pl.ds(bottom_start + begin, size)])
            return mm3(first, (high[:W], low[:W])) + mm3(second, (high[W:], low[W:]))

        if places[0][0] >= rolled[1]:
            @pl.loop(0, rows // rolled[0])
            def _(step):
                begin = pl.multiple_of(step * rolled[0], rolled[0])
                block = work(begin, rolled[0])
                for out, start in places:
                    held[out][pl.ds(start + begin, rolled[0])] = block
        else:
            for begin in range(0, rows, BLOCK):
                block = work(begin, BLOCK)
                for out, start in places:
                    held[out][start + begin:start + begin + BLOCK] = block
        for out, start in places:
            if to_hbm[out]:
                span, sems = pl.ds(start, rows), scratch[2 * sum(to_hbm[:out]) + 1]
                copies.append(pltpu.make_async_copy(held[out].at[span], outs[out].at[span], sems.at[len(copies)]))
                copies[-1].start()
    for source, start, rows, out, out_start in moves:
        held[out][out_start:out_start + rows] = refs[source][start:start + rows]
    for copy in copies:
        copy.wait()


def rotated(jobs, outs, moves=(), after=(), rolled=(BLOCK, 9)):
    arrays, turns = [], []

    def index(array, known):
        for idx, other in enumerate(known):
            if other is array:
                return idx
        known.append(array)
        return len(known) - 1

    listed, count = [], 0
    for top, top_start, bottom, bottom_start, rows, turn, places in jobs:
        count += rows
        listed.append((index(top, arrays), top_start, index(bottom, arrays), bottom_start, rows, index(turn, turns),
                       tuple(places)))
    copied = [(index(array, arrays), start, rows, out, row) for array, start, rows, out, row in moves]
    scratch = []
    for rows, hbm in outs:
        if hbm:
            scratch += [pltpu.VMEM((rows, W), F32), pltpu.SemaphoreType.DMA((8,))]
    result = pl.pallas_call(
        functools.partial(apply_kernel, listed, copied, len(arrays), len(turns), len(after), [hbm for _, hbm in outs], rolled),
        out_shape=[jax.ShapeDtypeStruct((rows, W), F32) for rows, _ in outs],
        in_specs=[IN_VMEM] * (len(arrays) + len(turns)) + [ANYWHERE] * len(after),
        out_specs=[IN_HBM if hbm else IN_VMEM for _, hbm in outs],
        scratch_shapes=scratch,
        compiler_params=granted(12),
        cost_estimate=pl.CostEstimate(flops=6 * 2 * W * W * count, bytes_accessed=12 * W * count, transcendentals=0),
    )(*arrays, *turns, *after)
    return result


def sum_kernel(count, *refs):
    refs[-1][...] = functools.reduce(lambda a, b: a + b, [ref[...] for ref in refs[:count]])


def summed(terms, after):
    return pl.pallas_call(
        functools.partial(sum_kernel, len(terms)),
        out_shape=jax.ShapeDtypeStruct(terms[0].shape, F32),
        in_specs=[IN_VMEM] * len(terms) + [ANYWHERE] * len(after),
        out_specs=IN_VMEM,
        compiler_params=granted(2),
    )(*terms, *after)


def tie_kernel(*refs):
    pass


def tied(array, after):
    return pl.pallas_call(
        tie_kernel,
        out_shape=jax.ShapeDtypeStruct(array.shape, F32),
        in_specs=[ANYWHERE] * (1 + len(after)),
        out_specs=ANYWHERE,
        input_output_aliases={0: 0},
        compiler_params=granted(1),
    )(array, *after)


def last_kernel(count, *refs):
    parts, out_ref, sems = refs[:count], refs[count + 1], refs[count + 2]
    at, copies = out_ref.shape[0], []
    for idx in reversed(range(count)):
        rows = parts[idx].shape[0]
        at -= rows
        copies.append(pltpu.make_async_copy(parts[idx], out_ref.at[pl.ds(at, rows)], sems.at[idx]))
        copies[-1].start()
    for copy in copies:
        copy.wait()


def with_last(whole, parts):
    return pl.pallas_call(
        functools.partial(last_kernel, len(parts)),
        out_shape=jax.ShapeDtypeStruct(whole.shape, F32),
        in_specs=[IN_VMEM] * len(parts) + [IN_HBM],
        out_specs=IN_HBM,
        scratch_shapes=[pltpu.SemaphoreType.DMA((len(parts),))],
        input_output_aliases={len(parts): 0},
        compiler_params=granted(2),
    )(*parts, whole)


def passed_along(array, by=1):
    length = lax.axis_size("pair")
    return lax.ppermute(array, "pair", [(i, (i + by) % length) for i in range(length)])


def along_y(array, by):
    length = lax.axis_size("row") // 2
    return lax.ppermute(
        array, "row", [(2 * y + h, 2 * ((y + by) % length) + h) for y in range(length) for h in range(2)]
    )


def across_x(array):
    return lax.ppermute(array, "row", [(i, i ^ 1) for i in range(lax.axis_size("row"))])


def scattered(pieces, after):
    return summed([pieces[0]] + [along_y(pieces[r], r) for r in (1, 2, 3)], after)


def gathered_quarters(total):
    return [total] + [along_y(total, r) for r in (1, 2, 3)]


def on_device(top, bottom):
    where = (lax.axis_index("row") // 2).astype(jnp.int32).reshape(1)
    rows = top.shape[0]
    late = rows - RAW
    mid = late - LAST

    own_a = loaded(top, bottom, RAW)
    raw = passed_along(own_a)
    *pieces, own_b = first_gram(where, own_a, top, bottom)
    total = scattered(pieces, [])
    total = summed([total, across_x(total)], [raw])
    total_prev = passed_along(total)
    first, second, whole = rotation(where, gathered_quarters(total))
    (sent,) = rotated([(own_b, 0, own_b, late, late, first, [(0, 0)])], [(late, False)], after=[total_prev], rolled=(512, 0))
    quarters_prev = gathered_quarters(tied(total_prev, [sent]))
    sent = passed_along(sent)
    (bottom,) = rotated(
        [(own_a, 0, own_a, RAW, RAW, second, [(0, 0)]), (own_b, 0, own_b, late, late, second, [(0, RAW)])],
        [(rows, False)],
        rolled=(BLOCK, 0),
    )
    (bottom_gram,) = turned_grams(whole, second)
    first_prev, second_prev, whole_prev = rotation(where, quarters_prev, [bottom_gram])
    (early,) = rotated(
        [(raw, 0, raw, RAW, RAW, first_prev, [(0, 0)])], [(RAW + MORE, False)], [(bottom, RAW, MORE, 0, RAW)],
        rolled=(BLOCK, 0),
    )
    early_prev = passed_along(early)
    (top_gram,) = turned_grams(whole_prev, first_prev)

    *pieces, ship = late_cross(
        where, sent, bottom, early_cross(early, bottom), mid, []
    )
    total = scattered(pieces, [early_prev, top_gram])
    total = total + across_x(total)
    ship = passed_along(tied(ship, [total]))
    (bottom_prev,) = rotated(
        [(raw, 0, raw, RAW, RAW, second_prev, [(0, 0)])], [(RAW, False)], rolled=(BLOCK, 0)
    )
    first, second = second_rotation(where, gathered_quarters(total), top_gram, bottom_gram)
    first_prev = passed_along(first)
    *out_late, bottom_out = rotated(
        [
            (sent, mid, bottom, RAW + mid, LAST - W, first, [(0, 0)]),
            (sent, late - W, bottom, rows - W, W, first, [(1, 0)]),
            (early, 0, bottom, 0, RAW, second, [(2, 0)]),
            (sent, 0, bottom, RAW, late, second, [(2, RAW)]),
        ],
        [(LAST - W, False), (W, False), (rows, True)],
        rolled=(BLOCK, 2),
    )
    out_late = [passed_along(part) for part in out_late]
    (top_out,) = rotated(
        [
            (early_prev, 0, bottom_prev, 0, RAW, first_prev, [(0, 0)]),
            (ship, 0, early_prev, RAW, MORE, first_prev, [(0, RAW)]),
            (ship, MORE, ship, mid, mid - MORE, first_prev, [(0, RAW + MORE)]),
        ],
        [(rows, True)],
        rolled=(BLOCK, 0),
    )
    return (with_last(top_out, out_late), bottom_out)


def solution(mesh):
    placed = (P("row", "pair"), P("row", "pair"))
    return jax.shard_map(on_device, mesh=mesh, in_specs=placed, out_specs=placed, check_vma=False)
```
